128 devices in a mesh: seg: 8 (over z, core), energy: 16 (over y, x).
Axes of the slice: x: 4, y: 4, z: 4, core: 2. Of those that a mesh axis runs over, the one named last changes fastest.
Arguments:
- green: float32 [16, 32, 2, 256, 256], P('energy', 'seg'), may hold values from -6 to 6
- couple_left: float32 [16, 32, 2, 256, 256], P('energy', 'seg'), may hold values from -0.01171875 to 0.01171875
- couple_right: float32 [16, 32, 2, 256, 256], P('energy', 'seg'), may hold values from -0.01171875 to 0.01171875
- coupling: int32 [16, 32], P('energy', 'seg'), may hold values 0 or 1
- screened: float32 [16, 32, 2, 256, 256], P('energy', 'seg'), may hold values from -1.5 to 1.5
Outputs:
- diagonal: float32 [16, 32, 2, 256, 256], P('energy', 'seg')
- self_energy: float32 [16, 32, 2, 256, 256], P('energy', 'seg')
The draws below stay inside these ranges and needn't reach their ends.
Inputs may be any that keep to these rules, and one draw needn't show every extreme that they name: `coupling`: 1 where block b is coupled to block b - 1, else 0; the entries of block 0 are not read.
All inputs are finite; a program needn't handle non-finite values.
Results may differ from the reference program's by a relative error of at most 0.0003.
Values sent between devices are 32-bit elements; how exact they have to be, the bound alone decides.
A program may use at most 128 MiB of HBM per device.

```python
import jax
import jax.numpy as jnp
from jax import lax

B = 256
NE = 16
NB = 32


def with_ends(values, own_key, low, high):
    extent = values.shape
    spot = [jax.random.randint(jax.random.fold_in(own_key, axis), (), 0, extent[axis]) for axis in range(len(extent))]
    values = values.at[tuple(spot)].set(low)
    longest = extent.index(max(extent))
    spot[longest] = (spot[longest] + 1) % extent[longest]
    return values.at[tuple(spot)].set(high)


def steps_of(stream_key, shape, shards, least, top_value):
    def one(position, shards_of):
        draws = jax.random.uniform(jax.random.fold_in(jax.random.fold_in(stream_key, 6), position), (shards_of,), jnp.float32, least / len(shards), top_value / len(shards))
        return jnp.repeat(jnp.exp(draws), shape[position] // shards_of).reshape((-1,) + (1,) * (len(shape) - position - 1))

    factor_of = one(*shards[0])
    for cut in shards[1:]:
        factor_of = factor_of * one(*cut)
    return factor_of


def centred(own_key, shape, width, bound, shards=(), dtype=jnp.bfloat16):
    gain = steps_of(own_key, shape, shards, -0.22, 0.18) if shards else 1.0
    values = jax.random.normal(own_key, shape, jnp.float32) * width * gain
    return jnp.minimum(jnp.maximum(values, -bound), bound).astype(dtype)


def setup_inputs(seed: int = 0) -> dict:
    key_list = jax.random.split(jax.random.key(seed), 6)
    return {
        "green": centred(key_list[0], (NE, NB, 2, B, B), 1.0, 6.0, ((0, 16), (1, 8)), jnp.float32),
        "couple_left": centred(key_list[1], (NE, NB, 2, B, B), (4 * B * B) ** -0.5, 0.01171875, ((0, 16), (1, 8)), jnp.float32),
        "couple_right": centred(key_list[2], (NE, NB, 2, B, B), (4 * B * B) ** -0.5, 0.01171875, ((0, 16), (1, 8)), jnp.float32),
        "coupling": with_ends((jax.random.randint(key_list[3], (NE, NB), 0, 16) < 15).astype(jnp.int32), jax.random.fold_in(key_list[3], 1), 0, 1),
        "screened": centred(key_list[4], (NE, NB, 2, B, B), NE ** -0.5, 1.5, ((0, 16), (1, 8)), jnp.float32),
    }


def real_product(left_part, right_part):
    return jnp.einsum('...ij,...jk->...ik', left_part, right_part, precision=lax.Precision.HIGHEST)


def complex_product(first, second):
    first_real, first_imag = first[..., 0, :, :], first[..., 1, :, :]
    second_real, second_imag = second[..., 0, :, :], second[..., 1, :, :]
    real_part = real_product(first_real, second_real) - real_product(first_imag, second_imag)
    imag_part = real_product(first_real, second_imag) + real_product(first_imag, second_real)
    return jnp.stack([real_part, imag_part], axis=-3)


def entry_product(first, second):
    first_real, first_imag = first[..., 0, :, :], first[..., 1, :, :]
    second_real, second_imag = second[..., 0, :, :], second[..., 1, :, :]
    return jnp.stack([first_real * second_real - first_imag * second_imag,
                      first_real * second_imag + first_imag * second_real], axis=-3)


def reference(green, couple_left, couple_right, coupling, screened):
    green_blocks = jnp.moveaxis(green, 1, 0)
    left_blocks = jnp.moveaxis(couple_left, 1, 0)
    right_blocks = jnp.moveaxis(couple_right, 1, 0)
    weights = jnp.moveaxis(coupling.astype(jnp.float32), 1, 0)[:, :, None, None, None]
    zero_block = jnp.zeros(green_blocks.shape[1:], jnp.float32)

    def forward(previous, inputs):
        block_green, block_left, block_right, weight = inputs
        fresh = block_green + weight * complex_product(
            complex_product(complex_product(block_green, block_left), previous),
            complex_product(block_right, block_green))
        return fresh, fresh

    def backward(following, inputs):
        block_green, block_left, block_right, weight = inputs
        dressed = complex_product(complex_product(block_green, following), block_green)
        outgoing = weight * complex_product(complex_product(block_right, block_green + dressed), block_left)
        return outgoing, dressed

    inputs = (green_blocks, left_blocks, right_blocks, weights)
    _, lefts = lax.scan(forward, zero_block, inputs)
    _, dressings = lax.scan(backward, zero_block, inputs, reverse=True)
    diagonal = jnp.moveaxis(lefts + dressings, 0, 1)

    def accumulate(offset, summed):
        rolled = jnp.roll(diagonal, offset, axis=0)
        factor = lax.dynamic_index_in_dim(screened, offset, 0, keepdims=True)
        return summed + entry_product(rolled, factor)

    self_energy = lax.fori_loop(0, NE, accumulate, jnp.zeros(diagonal.shape, jnp.float32))
    return diagonal, self_energy
```

```python
import functools
import math

import jax
import jax.numpy as jnp
from jax import lax
from jax.experimental import pallas as pl
from jax.experimental.pallas import tpu as pltpu
from jax.sharding import PartitionSpec as P

F32 = jnp.float32
BF16 = jnp.bfloat16
MESH = pl.DeviceIdType.MESH

G0, X0, Y0, Z3 = 3, 10, 17, 21
T0, T1, A_IN, C_IN, RS, RP, RQ, U, W, M_IN, CUR = range(25, 36)
PLACES = 36
BLOCKS = 4


def dft(values):
    n = len(values)
    if n == 1:
        return values
    even, odd = dft(values[0::2]), dft(values[1::2])
    out = [None] * n
    half = n // 2
    for j in range(half):
        er, ei = even[j]
        orr, oi = odd[j]
        angle = -2.0 * math.pi * j / n
        cos, sin = math.cos(angle), math.sin(angle)
        if j == 0:
            tr, ti = orr, oi
        elif 4 * j == n:
            tr, ti = oi, -orr
        elif 8 * j == n:
            tr, ti = (orr + oi) * cos, (oi - orr) * cos
        elif 8 * j == 3 * n:
            tr, ti = (oi - orr) * -cos, (orr + oi) * cos
        else:
            tr, ti = orr * cos - oi * sin, orr * sin + oi * cos
        out[j] = (er + tr, ei + ti)
        out[j + half] = (er - tr, ei - ti)
    return out


def kernel(
    ny, nx,
    g_hbm, a_hbm, c_hbm, m_ref, w_hbm, diag_hbm, self_hbm,
    gf, af, cf, zf, sf, pqf, rx, co, mi, oi, dg, rows, srows, res, ops,
    in_sem, sc_sem, x_send, x_recv, ch_sem, fw_sem, a_send, a_recv, r_send, r_recv, out_sem,
):
    ne = ny * nx
    depth = dg.shape[2] // ne
    width = dg.shape[3]
    seg = lax.axis_index("seg")
    me = lax.axis_index("energy")
    z, c = lax.div(seg, 2), lax.rem(seg, 2)
    nz = lax.axis_size("seg") // 2
    last = nz - 1
    my_y, my_x = lax.div(me, nx), lax.rem(me, nx)
    k = c * z + (1 - c) * (last - z)
    partner = seg + 1 - 2 * c
    onward = seg + 4 * c - 2
    high = lax.div(2 * z, nz)

    def peer(offset):
        dy, dx = lax.div(offset, nx), lax.rem(offset, nx)
        return lax.rem(my_y + dy, ny) * nx + lax.rem(my_x + dx, nx)

    def rows_of(energy):
        return pl.ds(pl.multiple_of(energy * depth, depth), depth)

    def load(b):
        return [
            pltpu.make_async_copy(src.at[b], dst.at[b], in_sem.at[b, j])
            for j, (src, dst) in enumerate(((g_hbm, gf), (a_hbm, af), (c_hbm, cf)))
        ]

    for b in range(BLOCKS):
        for copy in load(b):
            copy.start()

    barrier = pltpu.get_barrier_semaphore()

    @pl.loop(1, ne)
    def _(offset):
        pl.semaphore_signal(barrier, inc=1, device_id=(seg, peer(offset)), device_id_type=MESH)

    pl.semaphore_signal(barrier, inc=1, device_id=(partner, me), device_id_type=MESH)

    @pl.when(z > 0)
    def _():
        pl.semaphore_signal(barrier, inc=1, device_id=(seg - 2, me), device_id_type=MESH)

    @pl.when(z < last)
    def _():
        pl.semaphore_signal(barrier, inc=1, device_id=(seg + 2, me), device_id_type=MESH)

    neighbours = lax.div(z + last, nz) + lax.div(last - z + last, nz)
    pl.semaphore_wait(barrier, ne + neighbours)

    @pl.loop(1, ne)
    def _(offset):
        to = peer(offset)
        pltpu.make_async_remote_copy(
            src_ref=w_hbm.at[:, :, rows_of(to), :],
            dst_ref=srows.at[me],
            send_sem=sc_sem.at[0],
            recv_sem=sc_sem.at[1],
            device_id=(seg, to),
            device_id_type=MESH,
        ).start()

    own_screen = pltpu.make_async_copy(w_hbm.at[:, :, rows_of(me), :], srows.at[me], sc_sem.at[2])
    own_screen.start()

    def split_store(place, real, imag):
        for q, value in enumerate((real, imag, real + imag)):
            top = value.astype(BF16)
            ops[place, q, 0] = top
            ops[place, q, 1] = (value - top.astype(F32)).astype(BF16)

    def product(left, right):
        parts = []
        for q in range(3):
            lhs = jnp.concatenate([ops[left, q, 0], ops[left, q, 0], ops[left, q, 1]], axis=1)
            rhs = jnp.concatenate([ops[right, q, 0], ops[right, q, 1], ops[right, q, 0]], axis=0)
            parts.append(jnp.dot(lhs, rhs, preferred_element_type=F32))
        return parts[0] - parts[1], parts[2] - parts[0] - parts[1]

    @pl.loop(0, BLOCKS)
    def _(b):
        for copy in load(b):
            copy.wait()
        weight = m_ref[0, b].astype(F32)
        split_store(G0 - b, gf[b, 0], gf[b, 1])
        split_store(A_IN, af[b, 0] * weight, af[b, 1] * weight)
        split_store(C_IN, cf[b, 0], cf[b, 1])
        split_store(X0 - b, *product(G0 - b, A_IN))
        split_store(Y0 - b, *product(C_IN, G0 - b))
        real, imag = product(C_IN, X0 - b)
        zf[b, 0] = real
        zf[b, 1] = imag

        @pl.when(b == BLOCKS - 1)
        def _():
            split_store(Z3, zf[BLOCKS - 1, 0], zf[BLOCKS - 1, 1])

    @pl.loop(1, BLOCKS)
    def _(i):
        j = BLOCKS - 1 - i
        split_store(T0, *product(X0 - i, G0 + i - 1))
        split_store(T1, *product(Y0 - j, Z3 + i - 1))
        real, imag = product(T0, Y0 - i)
        real, imag = real + gf[i, 0], imag + gf[i, 1]
        sf[0, 0] = real
        sf[0, 1] = imag
        split_store(G0 + i, real, imag)
        real, imag = product(T1, X0 - j)
        real, imag = real + zf[j, 0], imag + zf[j, 1]
        sf[1, 0] = real
        sf[1, 1] = imag
        split_store(Z3 + i, real, imag)

    def exchange(j, src):
        return pltpu.make_async_remote_copy(
            src_ref=src,
            dst_ref=rx.at[j],
            send_sem=x_send.at[j],
            recv_sem=x_recv.at[j],
            device_id=(partner, me),
            device_id_type=MESH,
        )

    swap_source = exchange(0, sf.at[c])
    swap_source.start()

    @pl.loop(1, BLOCKS)
    def _(i):
        real, imag = product(X0 - i, X0 + i - 1)
        pqf[0, 0] = real
        pqf[0, 1] = imag
        split_store(X0 + i, real, imag)
        real, imag = product(Y0 + i - 1, Y0 - i)
        pqf[1, 0] = real
        pqf[1, 1] = imag
        split_store(Y0 + i, real, imag)

    swap_p, swap_q = exchange(1, pqf.at[0]), exchange(2, pqf.at[1])
    swap_p.start()
    swap_q.start()

    own_p, own_q = X0 + BLOCKS - 1, Y0 + BLOCKS - 1
    own_left = c * own_p + (1 - c) * own_q
    own_right = c * own_q + (1 - c) * own_p
    his_left = RP + 1 - c
    his_right = RP + c
    relay = pltpu.make_async_remote_copy(
        src_ref=co, dst_ref=mi, send_sem=ch_sem.at[0], recv_sem=ch_sem.at[1],
        device_id=(onward, me), device_id_type=MESH,
    )
    forward = pltpu.make_async_remote_copy(
        src_ref=mi, dst_ref=oi, send_sem=fw_sem.at[0], recv_sem=fw_sem.at[1],
        device_id=(partner, me), device_id_type=MESH,
    )

    swap_source.wait_recv()
    split_store(RS, rx[0, 0], rx[0, 1])
    split_store(T0, *product(own_left, RS))
    real, imag = product(T0, own_right)
    co[0] = real + sf[1 - c, 0]
    co[1] = imag + sf[1 - c, 1]

    @pl.when(k == 0)
    def _():
        relay.start()

    swap_p.wait_recv()
    swap_q.wait_recv()
    split_store(RP, rx[1, 0], rx[1, 1])
    split_store(RQ, rx[2, 0], rx[2, 1])
    split_store(U, *product(own_left, his_left))
    split_store(W, *product(his_right, own_right))

    def batch(b, sem):
        spot = rows.at[b, pl.ds(0, ne - 1)]
        return pltpu.make_async_copy(spot, spot, sem.at[b])

    def diag_out(b):
        return pltpu.make_async_copy(dg.at[b], diag_hbm.at[b], out_sem.at[0, b])

    def publish(second, b, real, imag):
        @pl.when(second == 0)
        def _():
            dg[b, 0] = real
            dg[b, 1] = imag

        @pl.when(second == 1)
        def _():
            dg[b, 0] = dg[b, 0] + real
            dg[b, 1] = dg[b, 1] + imag

            @pl.loop(1, ne)
            def _(offset):
                to = peer(offset)
                pltpu.make_async_remote_copy(
                    src_ref=dg.at[b, :, rows_of(to), :],
                    dst_ref=rows.at[b, me],
                    send_sem=a_send.at[b],
                    recv_sem=a_recv.at[b],
                    device_id=(seg, to),
                    device_id_type=MESH,
                ).start()

            diag_out(b).start()
            rows[b, me] = dg[b, :, rows_of(me), :]

    tiles = [(r, v) for r in range(0, depth, 8) for v in range(0, width, 128)]

    @pl.loop(0, 2)
    def _(i):
        direction = lax.rem(i + high, 2)
        own = lax.rem(direction + c, 2) == 1

        @pl.when(i == 1)
        def _():
            spot = srows.at[pl.ds(0, ne - 1)]
            pltpu.make_async_copy(spot, spot, sc_sem.at[1]).wait()
            own_screen.wait()

            @pl.loop(0, BLOCKS)
            def _(b):
                for r, v in tiles:
                    at = (pl.ds(r, 8), pl.ds(v, 128))
                    values = dft([(srows[(e, b, 0) + at], srows[(e, b, 1) + at]) for e in range(ne)])
                    for e in range(ne):
                        srows[(e, b, 0) + at] = values[e][0] * (1.0 / ne)
                        srows[(e, b, 1) + at] = values[e][1] * (1.0 / ne)

        @pl.when((i == lax.div(k, last)) & (k > 0))
        def _():
            relay.wait_recv()
            forward.start()
            split_store(M_IN, mi[0], mi[1])

            @pl.when(k < last)
            def _():
                split_store(T0, *product(U, M_IN))
                real, imag = product(T0, W)
                co[0] = co[0] + real
                co[1] = co[1] + imag
                relay.start()

        @pl.when(own & (k > 0))
        def _():
            split_store(T0, *product(his_left, M_IN))
            real, imag = product(T0, his_right)
            split_store(CUR, real + rx[0, 0], imag + rx[0, 1])

        @pl.when(own & (k == 0))
        def _():
            split_store(CUR, rx[0, 0], rx[0, 1])

        @pl.when(jnp.logical_not(own) & (k < last))
        def _():
            forward.wait_recv()
            split_store(CUR, oi[0], oi[1])

        @pl.when(jnp.logical_not(own) & (k == last))
        def _():
            ops[CUR] = jnp.zeros(ops.shape[1:], BF16)

        @pl.when(direction == 0)
        def _():
            @pl.loop(0, BLOCKS)
            def _(b):
                split_store(T0, *product(X0 - b, CUR))
                real, imag = product(T0, Y0 - b)
                real, imag = real + gf[b, 0], imag + gf[b, 1]
                publish(i, b, real, imag)
                split_store(CUR, real, imag)

        @pl.when(direction == 1)
        def _():
            @pl.loop(0, BLOCKS)
            def _(j):
                b = BLOCKS - 1 - j
                split_store(T0, *product(G0 - b, CUR))
                real, imag = product(T0, G0 - b)
                publish(i, b, real, imag)

                @pl.when(b > 0)
                def _():
                    split_store(T1, *product(Y0 - b, CUR))
                    real, imag = product(T1, X0 - b)
                    split_store(CUR, real + zf[b, 0], imag + zf[b, 1])

    def own_self(b):
        return pltpu.make_async_copy(
            res.at[b, me], self_hbm.at[b, :, rows_of(me), :], out_sem.at[1, b]
        )

    @pl.loop(0, BLOCKS)
    def _(j):
        b = high * j + (1 - high) * (BLOCKS - 1 - j)
        batch(b, a_recv).wait()
        for r, v in tiles:
            at = (pl.ds(r, 8), pl.ds(v, 128))
            values = dft([(rows[(b, e, 0) + at], rows[(b, e, 1) + at]) for e in range(ne)])
            mixed = []
            for e in range(ne):
                vr, vi = values[e]
                wr, wi = srows[(e, b, 0) + at], srows[(e, b, 1) + at]
                mixed.append((vr * wi + vi * wr, vr * wr - vi * wi))
            values = dft(mixed)
            for e in range(ne):
                res[(b, e, 0) + at] = values[e][1]
                res[(b, e, 1) + at] = values[e][0]

        @pl.loop(1, ne)
        def _(offset):
            to = peer(offset)
            pltpu.make_async_remote_copy(
                src_ref=res.at[b, to],
                dst_ref=self_hbm.at[b, :, rows_of(me), :],
                send_sem=r_send.at[b],
                recv_sem=r_recv.at[b],
                device_id=(seg, to),
                device_id_type=MESH,
            ).start()

        own_self(b).start()

    @pl.loop(0, BLOCKS)
    def _(b):
        for sem in (a_send, r_send, r_recv):
            batch(b, sem).wait()
        diag_out(b).wait()
        own_self(b).wait()

    spot = srows.at[pl.ds(0, ne - 1)]
    pltpu.make_async_copy(spot, spot, sc_sem.at[0]).wait()
    swap_source.wait_send()
    swap_p.wait_send()
    swap_q.wait_send()

    @pl.when(k < last)
    def _():
        relay.wait_send()

    @pl.when(k > 0)
    def _():
        forward.wait_send()


def per_device(ny, nx, green, couple_left, couple_right, coupling, screened):
    shape = green.shape[1:]
    blocks, _, order, _ = shape
    ne = ny * nx
    depth = order // ne
    one = (2, order, order)
    anywhere = pl.BlockSpec(memory_space=pl.ANY)
    diagonal, self_energy = pl.pallas_call(
        functools.partial(kernel, ny, nx),
        out_shape=[jax.ShapeDtypeStruct(shape, F32)] * 2,
        in_specs=[anywhere] * 3 + [pl.BlockSpec(memory_space=pltpu.SMEM), anywhere],
        out_specs=[anywhere] * 2,
        scratch_shapes=[
            pltpu.VMEM(shape, F32),
            pltpu.VMEM(shape, F32),
            pltpu.VMEM(shape, F32),
            pltpu.VMEM(shape, F32),
            pltpu.VMEM((2,) + one, F32),
            pltpu.VMEM((2,) + one, F32),
            pltpu.VMEM((3,) + one, F32),
            pltpu.VMEM(one, F32),
            pltpu.VMEM(one, F32),
            pltpu.VMEM(one, F32),
            pltpu.VMEM(shape, F32),
            pltpu.VMEM((blocks, ne, 2, depth, order), F32),
            pltpu.VMEM((ne, blocks, 2, depth, order), F32),
            pltpu.VMEM((blocks, ne, 2, depth, order), F32),
            pltpu.VMEM((PLACES, 3, 2, order, order), BF16),
            pltpu.SemaphoreType.DMA((blocks, 3)),
            pltpu.SemaphoreType.DMA((3,)),
            pltpu.SemaphoreType.DMA((3,)),
            pltpu.SemaphoreType.DMA((3,)),
            pltpu.SemaphoreType.DMA((2,)),
            pltpu.SemaphoreType.DMA((2,)),
            pltpu.SemaphoreType.DMA((blocks,)),
            pltpu.SemaphoreType.DMA((blocks,)),
            pltpu.SemaphoreType.DMA((blocks,)),
            pltpu.SemaphoreType.DMA((blocks,)),
            pltpu.SemaphoreType.DMA((2, blocks)),
        ],
        compiler_params=pltpu.CompilerParams(
            collective_id=0, has_side_effects=True, vmem_limit_bytes=60 * 2**20
        ),
    )(green[0], couple_left[0], couple_right[0], coupling, screened[0])
    return diagonal[None], self_energy[None]


def solution(mesh):
    blocks = P("energy", "seg", None, None, None)
    energies = mesh.shape["energy"]
    nx = math.isqrt(energies)
    return jax.shard_map(
        functools.partial(per_device, energies // nx, nx),
        mesh=mesh,
        in_specs=(blocks, blocks, blocks, P("energy", "seg"), blocks),
        out_specs=(blocks, blocks),
        check_vma=False,
    )
```

```python
import functools
import math

import jax
import jax.numpy as jnp
from jax import lax
from jax.experimental import pallas as pl
from jax.experimental.pallas import tpu as pltpu
from jax.sharding import PartitionSpec as P

F32 = jnp.float32
BF16 = jnp.bfloat16
MESH = pl.DeviceIdType.MESH

G0, X0, Y0 = 3, 10, 17
T0, T1, A_IN, C_IN, RS, RP, RQ, U, W, M_IN, CUR = range(21, 32)
PLACES = 32
BLOCKS = 4


def dft(values):
    n = len(values)
    if n == 1:
        return values
    even, odd = dft(values[0::2]), dft(values[1::2])
    out = [None] * n
    half = n // 2
    for j in range(half):
        er, ei = even[j]
        orr, oi = odd[j]
        angle = -2.0 * math.pi * j / n
        cos, sin = math.cos(angle), math.sin(angle)
        if j == 0:
            tr, ti = orr, oi
        elif 4 * j == n:
            tr, ti = oi, -orr
        elif 8 * j == n:
            tr, ti = (orr + oi) * cos, (oi - orr) * cos
        elif 8 * j == 3 * n:
            tr, ti = (oi - orr) * -cos, (orr + oi) * cos
        else:
            tr, ti = orr * cos - oi * sin, orr * sin + oi * cos
        out[j] = (er + tr, ei + ti)
        out[j + half] = (er - tr, ei - ti)
    return out


def kernel(
    ny, nx,
    g_hbm, a_hbm, c_hbm, m_ref, w_hbm, diag_hbm, self_hbm,
    gf, af, cf, sf, pqf, rx, co, mi, oi, dg, rows, srows, res, ops,
    in_sem, sc_sem, x_send, x_recv, ch_sem, fw_sem, a_send, a_recv, r_send, r_recv, out_sem,
):
    ne = ny * nx
    depth = dg.shape[2] // ne
    width = dg.shape[3]
    seg = lax.axis_index("seg")
    me = lax.axis_index("energy")
    z, c = lax.div(seg, 2), lax.rem(seg, 2)
    nz = lax.axis_size("seg") // 2
    last = nz - 1
    my_y, my_x = lax.div(me, nx), lax.rem(me, nx)
    k = c * z + (1 - c) * (last - z)
    partner = seg + 1 - 2 * c
    onward = seg + 4 * c - 2
    high = lax.div(2 * z, nz)

    def peer(offset):
        dy, dx = lax.div(offset, nx), lax.rem(offset, nx)
        return lax.rem(my_y + dy, ny) * nx + lax.rem(my_x + dx, nx)

    def rows_of(energy):
        return pl.ds(pl.multiple_of(energy * depth, depth), depth)

    def load(b):
        return [
            pltpu.make_async_copy(src.at[b], dst.at[b], in_sem.at[b, j])
            for j, (src, dst) in enumerate(((g_hbm, gf), (a_hbm, af), (c_hbm, cf)))
        ]

    for b in range(BLOCKS):
        for copy in load(b):
            copy.start()

    barrier = pltpu.get_barrier_semaphore()

    @pl.loop(1, ne)
    def _(offset):
        pl.semaphore_signal(barrier, inc=1, device_id=(seg, peer(offset)), device_id_type=MESH)

    pl.semaphore_signal(barrier, inc=1, device_id=(partner, me), device_id_type=MESH)

    @pl.when(z > 0)
    def _():
        pl.semaphore_signal(barrier, inc=1, device_id=(seg - 2, me), device_id_type=MESH)

    @pl.when(z < last)
    def _():
        pl.semaphore_signal(barrier, inc=1, device_id=(seg + 2, me), device_id_type=MESH)

    neighbours = lax.div(z + last, nz) + lax.div(last - z + last, nz)
    pl.semaphore_wait(barrier, ne + neighbours)

    @pl.loop(1, ne)
    def _(offset):
        to = peer(offset)
        pltpu.make_async_remote_copy(
            src_ref=w_hbm.at[:, :, rows_of(to), :],
            dst_ref=srows.at[me],
            send_sem=sc_sem.at[0],
            recv_sem=sc_sem.at[1],
            device_id=(seg, to),
            device_id_type=MESH,
        ).start()

    own_screen = pltpu.make_async_copy(w_hbm.at[:, :, rows_of(me), :], srows.at[me], sc_sem.at[2])
    own_screen.start()

    def split_store(place, real, imag):
        for q, value in enumerate((real, imag, real + imag)):
            top = value.astype(BF16)
            ops[place, q, 0] = top
            ops[place, q, 1] = (value - top.astype(F32)).astype(BF16)

    def product(left, right):
        parts = []
        for q in range(3):
            lhs = jnp.concatenate([ops[left, q, 0], ops[left, q, 0], ops[left, q, 1]], axis=1)
            rhs = jnp.concatenate([ops[right, q, 0], ops[right, q, 1], ops[right, q, 0]], axis=0)
            parts.append(jnp.dot(lhs, rhs, preferred_element_type=F32))
        return parts[0] - parts[1], parts[2] - parts[0] - parts[1]

    @pl.loop(0, BLOCKS)
    def _(b):
        for copy in load(b):
            copy.wait()
        weight = m_ref[0, b].astype(F32)
        af[b] = af[b] * weight
        split_store(G0 - b, gf[b, 0], gf[b, 1])
        split_store(A_IN, af[b, 0], af[b, 1])
        split_store(C_IN, cf[b, 0], cf[b, 1])
        split_store(X0 - b, *product(G0 - b, A_IN))
        split_store(Y0 - b, *product(C_IN, G0 - b))

    def exchange(j, src):
        return pltpu.make_async_remote_copy(
            src_ref=src,
            dst_ref=rx.at[j],
            send_sem=x_send.at[j],
            recv_sem=x_recv.at[j],
            device_id=(partner, me),
            device_id_type=MESH,
        )

    swap_source = exchange(0, sf.at[c])
    swap_p, swap_q = exchange(1, pqf.at[0]), exchange(2, pqf.at[1])

    own_p, own_q = X0 + BLOCKS - 1, Y0 + BLOCKS - 1
    own_left = c * own_p + (1 - c) * own_q
    own_right = c * own_q + (1 - c) * own_p
    his_left = RP + 1 - c
    his_right = RP + c
    relay = pltpu.make_async_remote_copy(
        src_ref=co, dst_ref=mi, send_sem=ch_sem.at[0], recv_sem=ch_sem.at[1],
        device_id=(onward, me), device_id_type=MESH,
    )
    forward = pltpu.make_async_remote_copy(
        src_ref=mi, dst_ref=oi, send_sem=fw_sem.at[0], recv_sem=fw_sem.at[1],
        device_id=(partner, me), device_id_type=MESH,
    )

    def chain(direction):
        @pl.when(direction == 0)
        def _():
            @pl.loop(1, BLOCKS)
            def _(b):
                split_store(T0, *product(X0 - b, G0 + b - 1))
                real, imag = product(T0, Y0 - b)
                real, imag = real + gf[b, 0], imag + gf[b, 1]
                sf[0, 0] = real
                sf[0, 1] = imag
                split_store(G0 + b, real, imag)

        @pl.when(direction == 1)
        def _():
            split_store(T1, af[BLOCKS - 1, 0], af[BLOCKS - 1, 1])

            @pl.loop(0, BLOCKS)
            def _(j):
                b = BLOCKS - 1 - j
                real, imag = product(Y0 - b, T1)
                sf[1, 0] = real
                sf[1, 1] = imag

                @pl.when(b > 0)
                def _():
                    split_store(CUR, real, imag)
                    real_next, imag_next = product(CUR, X0 - b + 1)
                    split_store(T1, real_next + af[b - 1, 0], imag_next + af[b - 1, 1])

        @pl.when(direction == c)
        def _():
            swap_source.start()

    def outer():
        @pl.loop(1, BLOCKS)
        def _(b):
            real, imag = product(X0 - b, X0 + b - 1)
            pqf[0, 0] = real
            pqf[0, 1] = imag
            split_store(X0 + b, real, imag)
            real, imag = product(Y0 + b - 1, Y0 - b)
            pqf[1, 0] = real
            pqf[1, 1] = imag
            split_store(Y0 + b, real, imag)

        swap_p.start()
        swap_q.start()

    def join():
        swap_source.wait_recv()
        split_store(RS, rx[0, 0], rx[0, 1])
        split_store(T0, *product(own_left, RS))
        real, imag = product(T0, own_right)
        co[0] = real + sf[1 - c, 0]
        co[1] = imag + sf[1 - c, 1]

        @pl.when(k == 0)
        def _():
            relay.start()

    def compose():
        swap_p.wait_recv()
        swap_q.wait_recv()
        split_store(RP, rx[1, 0], rx[1, 1])
        split_store(RQ, rx[2, 0], rx[2, 1])
        split_store(U, *product(own_left, his_left))
        split_store(W, *product(his_right, own_right))

    def batch(b, sem):
        spot = rows.at[b, pl.ds(0, ne - 1)]
        return pltpu.make_async_copy(spot, spot, sem.at[b])

    def diag_out(b):
        return pltpu.make_async_copy(dg.at[b], diag_hbm.at[b], out_sem.at[0, b])

    def publish(second, b, real, imag):
        @pl.when(second == 0)
        def _():
            dg[b, 0] = real
            dg[b, 1] = imag

        @pl.when(second == 1)
        def _():
            dg[b, 0] = dg[b, 0] + real
            dg[b, 1] = dg[b, 1] + imag

            @pl.loop(1, ne)
            def _(offset):
                to = peer(offset)
                pltpu.make_async_remote_copy(
                    src_ref=dg.at[b, :, rows_of(to), :],
                    dst_ref=rows.at[b, me],
                    send_sem=a_send.at[b],
                    recv_sem=a_recv.at[b],
                    device_id=(seg, to),
                    device_id_type=MESH,
                ).start()

            diag_out(b).start()
            rows[b, me] = dg[b, :, rows_of(me), :]

    tiles = [(r, v) for r in range(0, depth, 8) for v in range(0, width, 128)]

    def transform_screened():
        spot = srows.at[pl.ds(0, ne - 1)]
        pltpu.make_async_copy(spot, spot, sc_sem.at[1]).wait()
        own_screen.wait()

        @pl.loop(0, BLOCKS)
        def _(b):
            for r, v in tiles:
                at = (pl.ds(r, 8), pl.ds(v, 128))
                values = dft([(srows[(e, b, 0) + at], srows[(e, b, 1) + at]) for e in range(ne)])
                for e in range(ne):
                    srows[(e, b, 0) + at] = values[e][0] * (1.0 / ne)
                    srows[(e, b, 1) + at] = values[e][1] * (1.0 / ne)

    def pass_on():
        relay.wait_recv()
        forward.start()
        split_store(M_IN, mi[0], mi[1])

        @pl.when(k < last)
        def _():
            split_store(T0, *product(U, M_IN))
            real, imag = product(T0, W)
            co[0] = co[0] + real
            co[1] = co[1] + imag
            relay.start()

    def sweep(second, direction):
        own = lax.rem(direction + c, 2) == 1

        @pl.when(own & (k > 0))
        def _():
            split_store(T0, *product(his_left, M_IN))
            real, imag = product(T0, his_right)
            split_store(CUR, real + rx[0, 0], imag + rx[0, 1])

        @pl.when(own & (k == 0))
        def _():
            split_store(CUR, rx[0, 0], rx[0, 1])

        @pl.when(jnp.logical_not(own) & (k < last))
        def _():
            forward.wait_recv()
            split_store(CUR, oi[0], oi[1])

        @pl.when(jnp.logical_not(own) & (k == last))
        def _():
            ops[CUR] = jnp.zeros(ops.shape[1:], BF16)

        @pl.when(direction == 0)
        def _():
            @pl.loop(0, BLOCKS)
            def _(b):
                split_store(T0, *product(X0 - b, CUR))
                real, imag = product(T0, Y0 - b)
                real, imag = real + gf[b, 0], imag + gf[b, 1]
                publish(second, b, real, imag)
                split_store(CUR, real, imag)

        @pl.when(direction == 1)
        def _():
            @pl.loop(0, BLOCKS)
            def _(j):
                b = BLOCKS - 1 - j
                split_store(T0, *product(G0 - b, CUR))
                real, imag = product(T0, G0 - b)
                publish(second, b, real, imag)

                @pl.when(b > 0)
                def _():
                    real, imag = product(CUR, X0 - b)
                    split_store(T1, real + af[b, 0], imag + af[b, 1])
                    split_store(CUR, *product(Y0 - b, T1))

    @pl.loop(0, 4)
    def _(i):
        direction = lax.rem(i + high, 2)

        @pl.when(i == 3)
        def _():
            transform_screened()

        @pl.when((i == k) & (k > 0))
        def _():
            pass_on()

        @pl.when(i < 2)
        def _():
            chain(direction)

            @pl.when(i == 0)
            def _():
                outer()

            @pl.when(direction != c)
            def _():
                join()

            @pl.when(i == 0)
            def _():
                compose()

        @pl.when(i >= 2)
        def _():
            sweep(i - 2, direction)

    def own_self(b):
        return pltpu.make_async_copy(
            res.at[b, me], self_hbm.at[b, :, rows_of(me), :], out_sem.at[1, b]
        )

    @pl.loop(0, BLOCKS)
    def _(j):
        b = high * j + (1 - high) * (BLOCKS - 1 - j)
        batch(b, a_recv).wait()
        for r, v in tiles:
            at = (pl.ds(r, 8), pl.ds(v, 128))
            values = dft([(rows[(b, e, 0) + at], rows[(b, e, 1) + at]) for e in range(ne)])
            mixed = []
            for e in range(ne):
                vr, vi = values[e]
                wr, wi = srows[(e, b, 0) + at], srows[(e, b, 1) + at]
                mixed.append((vr * wi + vi * wr, vr * wr - vi * wi))
            values = dft(mixed)
            for e in range(ne):
                res[(b, e, 0) + at] = values[e][1]
                res[(b, e, 1) + at] = values[e][0]

        @pl.loop(1, ne)
        def _(offset):
            to = peer(offset)
            pltpu.make_async_remote_copy(
                src_ref=res.at[b, to],
                dst_ref=self_hbm.at[b, :, rows_of(me), :],
                send_sem=r_send.at[b],
                recv_sem=r_recv.at[b],
                device_id=(seg, to),
                device_id_type=MESH,
            ).start()

        own_self(b).start()

    @pl.loop(0, BLOCKS)
    def _(b):
        for sem in (a_send, r_send, r_recv):
            batch(b, sem).wait()
        diag_out(b).wait()
        own_self(b).wait()

    spot = srows.at[pl.ds(0, ne - 1)]
    pltpu.make_async_copy(spot, spot, sc_sem.at[0]).wait()
    swap_source.wait_send()
    swap_p.wait_send()
    swap_q.wait_send()

    @pl.when(k < last)
    def _():
        relay.wait_send()

    @pl.when(k > 0)
    def _():
        forward.wait_send()


def per_device(ny, nx, green, couple_left, couple_right, coupling, screened):
    shape = green.shape[1:]
    blocks, _, order, _ = shape
    ne = ny * nx
    depth = order // ne
    one = (2, order, order)
    anywhere = pl.BlockSpec(memory_space=pl.ANY)
    diagonal, self_energy = pl.pallas_call(
        functools.partial(kernel, ny, nx),
        out_shape=[jax.ShapeDtypeStruct(shape, F32)] * 2,
        in_specs=[anywhere] * 3 + [pl.BlockSpec(memory_space=pltpu.SMEM), anywhere],
        out_specs=[anywhere] * 2,
        scratch_shapes=[
            pltpu.VMEM(shape, F32),
            pltpu.VMEM(shape, F32),
            pltpu.VMEM(shape, F32),
            pltpu.VMEM((2,) + one, F32),
            pltpu.VMEM((2,) + one, F32),
            pltpu.VMEM((3,) + one, F32),
            pltpu.VMEM(one, F32),
            pltpu.VMEM(one, F32),
            pltpu.VMEM(one, F32),
            pltpu.VMEM(shape, F32),
            pltpu.VMEM((blocks, ne, 2, depth, order), F32),
            pltpu.VMEM((ne, blocks, 2, depth, order), F32),
            pltpu.VMEM((blocks, ne, 2, depth, order), F32),
            pltpu.VMEM((PLACES, 3, 2, order, order), BF16),
            pltpu.SemaphoreType.DMA((blocks, 3)),
            pltpu.SemaphoreType.DMA((3,)),
            pltpu.SemaphoreType.DMA((3,)),
            pltpu.SemaphoreType.DMA((3,)),
            pltpu.SemaphoreType.DMA((2,)),
            pltpu.SemaphoreType.DMA((2,)),
            pltpu.SemaphoreType.DMA((blocks,)),
            pltpu.SemaphoreType.DMA((blocks,)),
            pltpu.SemaphoreType.DMA((blocks,)),
            pltpu.SemaphoreType.DMA((blocks,)),
            pltpu.SemaphoreType.DMA((2, blocks)),
        ],
        compiler_params=pltpu.CompilerParams(
            collective_id=0, has_side_effects=True, vmem_limit_bytes=60 * 2**20
        ),
    )(green[0], couple_left[0], couple_right[0], coupling, screened[0])
    return diagonal[None], self_energy[None]


def solution(mesh):
    blocks = P("energy", "seg", None, None, None)
    energies = mesh.shape["energy"]
    nx = math.isqrt(energies)
    return jax.shard_map(
        functools.partial(per_device, energies // nx, nx),
        mesh=mesh,
        in_specs=(blocks, blocks, blocks, P("energy", "seg"), blocks),
        out_specs=(blocks, blocks),
        check_vma=False,
    )
```

```python
import functools
import math

import jax
import jax.numpy as jnp
from jax import lax
from jax.experimental import pallas as pl
from jax.experimental.pallas import tpu as pltpu
from jax.sharding import PartitionSpec as P

F32 = jnp.float32
BF16 = jnp.bfloat16
MESH = pl.DeviceIdType.MESH

G0, X0, Y0 = 3, 10, 17
T0, T1, A_IN, C_IN, RS, RP, RQ, U, W, M_IN, CUR = range(21, 32)
PLACES = 32
BLOCKS = 4


def dft(values):
    n = len(values)
    if n == 1:
        return values
    even, odd = dft(values[0::2]), dft(values[1::2])
    out = [None] * n
    half = n // 2
    for j in range(half):
        er, ei = even[j]
        orr, oi = odd[j]
        angle = -2.0 * math.pi * j / n
        cos, sin = math.cos(angle), math.sin(angle)
        if j == 0:
            tr, ti = orr, oi
        elif 4 * j == n:
            tr, ti = oi, -orr
        elif 8 * j == n:
            tr, ti = (orr + oi) * cos, (oi - orr) * cos
        elif 8 * j == 3 * n:
            tr, ti = (oi - orr) * -cos, (orr + oi) * cos
        else:
            tr, ti = orr * cos - oi * sin, orr * sin + oi * cos
        out[j] = (er + tr, ei + ti)
        out[j + half] = (er - tr, ei - ti)
    return out


def kernel(
    ny, nx,
    g_hbm, a_hbm, c_hbm, m_ref, w_hbm, diag_hbm, self_hbm,
    gf, af, cf, sf, pqf, rx, co, mi, oi, dg, rows, srows, res, ops,
    in_sem, sc_sem, x_send, x_recv, ch_sem, fw_sem, a_send, a_recv, r_send, r_recv, out_sem,
):
    ne = ny * nx
    depth = dg.shape[2] // ne
    width = dg.shape[3]
    seg = lax.axis_index("seg")
    me = lax.axis_index("energy")
    z, c = lax.div(seg, 2), lax.rem(seg, 2)
    nz = lax.axis_size("seg") // 2
    last = nz - 1
    my_y, my_x = lax.div(me, nx), lax.rem(me, nx)
    k = c * z + (1 - c) * (last - z)
    partner = seg + 1 - 2 * c
    onward = seg + 4 * c - 2
    high = lax.div(2 * z, nz)

    def peer(offset):
        dy, dx = lax.div(offset, nx), lax.rem(offset, nx)
        return lax.rem(my_y + dy, ny) * nx + lax.rem(my_x + dx, nx)

    def rows_of(energy):
        return pl.ds(pl.multiple_of(energy * depth, depth), depth)

    def load(b):
        return [
            pltpu.make_async_copy(src.at[b], dst.at[b], in_sem.at[b, j])
            for j, (src, dst) in enumerate(((g_hbm, gf), (a_hbm, af), (c_hbm, cf)))
        ]

    for b in range(BLOCKS):
        for copy in load(b):
            copy.start()

    barrier = pltpu.get_barrier_semaphore()

    @pl.loop(1, ne)
    def _(offset):
        pl.semaphore_signal(barrier, inc=1, device_id=(seg, peer(offset)), device_id_type=MESH)

    pl.semaphore_signal(barrier, inc=1, device_id=(partner, me), device_id_type=MESH)

    @pl.when(z > 0)
    def _():
        pl.semaphore_signal(barrier, inc=1, device_id=(seg - 2, me), device_id_type=MESH)

    @pl.when(z < last)
    def _():
        pl.semaphore_signal(barrier, inc=1, device_id=(seg + 2, me), device_id_type=MESH)

    neighbours = lax.div(z + last, nz) + lax.div(last - z + last, nz)
    pl.semaphore_wait(barrier, ne + neighbours)

    @pl.loop(1, ne)
    def _(offset):
        to = peer(offset)
        pltpu.make_async_remote_copy(
            src_ref=w_hbm.at[:, :, rows_of(to), :],
            dst_ref=srows.at[me],
            send_sem=sc_sem.at[0],
            recv_sem=sc_sem.at[1],
            device_id=(seg, to),
            device_id_type=MESH,
        ).start()

    own_screen = pltpu.make_async_copy(w_hbm.at[:, :, rows_of(me), :], srows.at[me], sc_sem.at[2])
    own_screen.start()

    def split_store(place, real, imag):
        for q, value in enumerate((real, imag, real + imag)):
            top = value.astype(BF16)
            ops[place, q, 0] = top
            ops[place, q, 1] = (value - top.astype(F32)).astype(BF16)

    def product(left, right):
        parts = []
        for q in range(3):
            lhs = jnp.concatenate([ops[left, q, 0], ops[left, q, 0], ops[left, q, 1]], axis=1)
            rhs = jnp.concatenate([ops[right, q, 0], ops[right, q, 1], ops[right, q, 0]], axis=0)
            parts.append(jnp.dot(lhs, rhs, preferred_element_type=F32))
        return parts[0] - parts[1], parts[2] - parts[0] - parts[1]

    dg[...] = jnp.zeros(dg.shape, F32)
    for b in range(BLOCKS):
        for copy in load(b):
            copy.wait()
        weight = m_ref[0, b].astype(F32)
        af[b] = af[b] * weight
        split_store(G0 - b, gf[b, 0], gf[b, 1])
        split_store(A_IN, af[b, 0], af[b, 1])
        split_store(C_IN, cf[b, 0], cf[b, 1])
        split_store(X0 - b, *product(G0 - b, A_IN))
        split_store(Y0 - b, *product(C_IN, G0 - b))

    def exchange(j, src):
        return pltpu.make_async_remote_copy(
            src_ref=src,
            dst_ref=rx.at[j],
            send_sem=x_send.at[j],
            recv_sem=x_recv.at[j],
            device_id=(partner, me),
            device_id_type=MESH,
        )

    swap_source = exchange(0, sf.at[c])
    swap_p, swap_q = exchange(1, pqf.at[0]), exchange(2, pqf.at[1])

    own_p, own_q = X0 + BLOCKS - 1, Y0 + BLOCKS - 1
    own_left = c * own_p + (1 - c) * own_q
    own_right = c * own_q + (1 - c) * own_p
    his_left = RP + 1 - c
    his_right = RP + c
    relay = pltpu.make_async_remote_copy(
        src_ref=co, dst_ref=mi, send_sem=ch_sem.at[0], recv_sem=ch_sem.at[1],
        device_id=(onward, me), device_id_type=MESH,
    )
    forward = pltpu.make_async_remote_copy(
        src_ref=mi, dst_ref=oi, send_sem=fw_sem.at[0], recv_sem=fw_sem.at[1],
        device_id=(partner, me), device_id_type=MESH,
    )

    def chain(direction, outer):
        for b in range(BLOCKS):
            j = BLOCKS - 1 - b
            if direction == 0 and b > 0:
                split_store(T0, *product(X0 - b, G0 + b - 1))
            if direction == 1 and b == 0:
                split_store(T1, af[j, 0], af[j, 1])
            if direction == 1 and b > 0:
                real, imag = product(CUR, X0 - j)
                split_store(T1, real + af[j, 0], imag + af[j, 1])
            if outer and b > 0:
                real, imag = product(X0 - b, X0 + b - 1)
                split_store(X0 + b, real, imag)
                if b == BLOCKS - 1:
                    pqf[0, 0] = real
                    pqf[0, 1] = imag
            if direction == 0 and b > 0:
                real, imag = product(T0, Y0 - b)
                real, imag = real + gf[b, 0], imag + gf[b, 1]
                if b < BLOCKS - 1:
                    split_store(G0 + b, real, imag)
            if direction == 1:
                real, imag = product(Y0 - j, T1)
                if b < BLOCKS - 1:
                    split_store(CUR, real, imag)
            if b == BLOCKS - 1:
                sf[direction, 0] = real
                sf[direction, 1] = imag
            if outer and b > 0:
                real, imag = product(Y0 + b - 1, Y0 - b)
                split_store(Y0 + b, real, imag)
                if b == BLOCKS - 1:
                    pqf[1, 0] = real
                    pqf[1, 1] = imag

        if outer:
            swap_p.start()
            swap_q.start()

        @pl.when(c == direction)
        def _():
            swap_source.start()

    def join():
        swap_source.wait_recv()
        split_store(RS, rx[0, 0], rx[0, 1])
        split_store(T0, *product(own_left, RS))
        real, imag = product(T0, own_right)
        co[0] = real + sf[1 - c, 0]
        co[1] = imag + sf[1 - c, 1]

        @pl.when(k == 0)
        def _():
            relay.start()

    def compose():
        swap_p.wait_recv()
        swap_q.wait_recv()
        split_store(RP, rx[1, 0], rx[1, 1])
        split_store(RQ, rx[2, 0], rx[2, 1])
        split_store(U, *product(own_left, his_left))
        split_store(W, *product(his_right, own_right))

    def batch(b, sem):
        spot = rows.at[b, pl.ds(0, ne - 1)]
        return pltpu.make_async_copy(spot, spot, sem.at[b])

    def diag_out(b):
        return pltpu.make_async_copy(dg.at[b], diag_hbm.at[b], out_sem.at[0, b])

    def publish(second, b, real, imag):
        dg[b, 0] = dg[b, 0] + real
        dg[b, 1] = dg[b, 1] + imag

        @pl.when(second == 1)
        def _():
            @pl.loop(1, ne)
            def _(offset):
                to = peer(offset)
                pltpu.make_async_remote_copy(
                    src_ref=dg.at[b, :, rows_of(to), :],
                    dst_ref=rows.at[b, me],
                    send_sem=a_send.at[b],
                    recv_sem=a_recv.at[b],
                    device_id=(seg, to),
                    device_id_type=MESH,
                ).start()

            diag_out(b).start()
            rows[b, me] = dg[b, :, rows_of(me), :]

    tiles = [(r, v) for r in range(0, depth, 8) for v in range(0, width, 128)]

    def transform_screened():
        spot = srows.at[pl.ds(0, ne - 1)]
        pltpu.make_async_copy(spot, spot, sc_sem.at[1]).wait()
        own_screen.wait()

        @pl.loop(0, BLOCKS)
        def _(b):
            for r, v in tiles:
                at = (pl.ds(r, 8), pl.ds(v, 128))
                values = dft([(srows[(e, b, 0) + at], srows[(e, b, 1) + at]) for e in range(ne)])
                for e in range(ne):
                    srows[(e, b, 0) + at] = values[e][0] * (1.0 / ne)
                    srows[(e, b, 1) + at] = values[e][1] * (1.0 / ne)

    def pass_on():
        relay.wait_recv()
        forward.start()
        split_store(M_IN, mi[0], mi[1])

        @pl.when(k < last)
        def _():
            split_store(T0, *product(U, M_IN))
            real, imag = product(T0, W)
            co[0] = co[0] + real
            co[1] = co[1] + imag
            relay.start()

    def sweep(second, direction):
        own = lax.rem(direction + c, 2) == 1

        @pl.when(own & (k > 0))
        def _():
            split_store(T0, *product(his_left, M_IN))
            real, imag = product(T0, his_right)
            split_store(CUR, real + rx[0, 0], imag + rx[0, 1])

        @pl.when(own & (k == 0))
        def _():
            split_store(CUR, rx[0, 0], rx[0, 1])

        @pl.when(jnp.logical_not(own) & (k < last))
        def _():
            forward.wait_recv()
            split_store(CUR, oi[0], oi[1])

        @pl.when(jnp.logical_not(own) & (k == last))
        def _():
            ops[CUR] = jnp.zeros(ops.shape[1:], BF16)

        @pl.when(direction == 0)
        def _():
            for b in range(BLOCKS):
                split_store(T0, *product(X0 - b, CUR))
                real, imag = product(T0, Y0 - b)
                real, imag = real + gf[b, 0], imag + gf[b, 1]
                if b < BLOCKS - 1:
                    split_store(CUR, real, imag)
                publish(second, b, real, imag)

        @pl.when(direction == 1)
        def _():
            for b in reversed(range(BLOCKS)):
                split_store(T0, *product(G0 - b, CUR))
                if b > 0:
                    real, imag = product(CUR, X0 - b)
                    split_store(T1, real + af[b, 0], imag + af[b, 1])
                publish(second, b, *product(T0, G0 - b))
                if b > 0:
                    split_store(CUR, *product(Y0 - b, T1))

    for i in range(2):
        if i == 1:
            @pl.when(k == 1)
            def _():
                pass_on()

        for side in range(2):
            @pl.when(high == side)
            def _():
                chain((i + side) % 2, i == 0)

        @pl.when(lax.rem(i + high + c, 2) == 1)
        def _():
            join()

        if i == 0:
            compose()

    @pl.loop(2, 4)
    def _(i):
        @pl.when(i == 3)
        def _():
            transform_screened()

        @pl.when(i == k)
        def _():
            pass_on()

        sweep(i - 2, lax.rem(i + high, 2))

    def own_self(b):
        return pltpu.make_async_copy(
            res.at[b, me], self_hbm.at[b, :, rows_of(me), :], out_sem.at[1, b]
        )

    @pl.loop(0, BLOCKS)
    def _(j):
        b = high * j + (1 - high) * (BLOCKS - 1 - j)
        batch(b, a_recv).wait()
        for r, v in tiles:
            at = (pl.ds(r, 8), pl.ds(v, 128))
            values = dft([(rows[(b, e, 0) + at], rows[(b, e, 1) + at]) for e in range(ne)])
            mixed = []
            for e in range(ne):
                vr, vi = values[e]
                wr, wi = srows[(e, b, 0) + at], srows[(e, b, 1) + at]
                mixed.append((vr * wi + vi * wr, vr * wr - vi * wi))
            values = dft(mixed)
            for e in range(ne):
                res[(b, e, 0) + at] = values[e][1]
                res[(b, e, 1) + at] = values[e][0]

        @pl.loop(1, ne)
        def _(offset):
            to = peer(offset)
            pltpu.make_async_remote_copy(
                src_ref=res.at[b, to],
                dst_ref=self_hbm.at[b, :, rows_of(me), :],
                send_sem=r_send.at[b],
                recv_sem=r_recv.at[b],
                device_id=(seg, to),
                device_id_type=MESH,
            ).start()

        own_self(b).start()

    @pl.loop(0, BLOCKS)
    def _(b):
        for sem in (a_send, r_send, r_recv):
            batch(b, sem).wait()
        diag_out(b).wait()
        own_self(b).wait()

    spot = srows.at[pl.ds(0, ne - 1)]
    pltpu.make_async_copy(spot, spot, sc_sem.at[0]).wait()
    swap_source.wait_send()
    swap_p.wait_send()
    swap_q.wait_send()

    @pl.when(k < last)
    def _():
        relay.wait_send()

    @pl.when(k > 0)
    def _():
        forward.wait_send()


def per_device(ny, nx, green, couple_left, couple_right, coupling, screened):
    shape = green.shape[1:]
    blocks, _, order, _ = shape
    ne = ny * nx
    depth = order // ne
    one = (2, order, order)
    anywhere = pl.BlockSpec(memory_space=pl.ANY)
    diagonal, self_energy = pl.pallas_call(
        functools.partial(kernel, ny, nx),
        out_shape=[jax.ShapeDtypeStruct(shape, F32)] * 2,
        in_specs=[anywhere] * 3 + [pl.BlockSpec(memory_space=pltpu.SMEM), anywhere],
        out_specs=[anywhere] * 2,
        scratch_shapes=[
            pltpu.VMEM(shape, F32),
            pltpu.VMEM(shape, F32),
            pltpu.VMEM(shape, F32),
            pltpu.VMEM((2,) + one, F32),
            pltpu.VMEM((2,) + one, F32),
            pltpu.VMEM((3,) + one, F32),
            pltpu.VMEM(one, F32),
            pltpu.VMEM(one, F32),
            pltpu.VMEM(one, F32),
            pltpu.VMEM(shape, F32),
            pltpu.VMEM((blocks, ne, 2, depth, order), F32),
            pltpu.VMEM((ne, blocks, 2, depth, order), F32),
            pltpu.VMEM((blocks, ne, 2, depth, order), F32),
            pltpu.VMEM((PLACES, 3, 2, order, order), BF16),
            pltpu.SemaphoreType.DMA((blocks, 3)),
            pltpu.SemaphoreType.DMA((3,)),
            pltpu.SemaphoreType.DMA((3,)),
            pltpu.SemaphoreType.DMA((3,)),
            pltpu.SemaphoreType.DMA((2,)),
            pltpu.SemaphoreType.DMA((2,)),
            pltpu.SemaphoreType.DMA((blocks,)),
            pltpu.SemaphoreType.DMA((blocks,)),
            pltpu.SemaphoreType.DMA((blocks,)),
            pltpu.SemaphoreType.DMA((blocks,)),
            pltpu.SemaphoreType.DMA((2, blocks)),
        ],
        compiler_params=pltpu.CompilerParams(
            collective_id=0, has_side_effects=True, vmem_limit_bytes=60 * 2**20
        ),
    )(green[0], couple_left[0], couple_right[0], coupling, screened[0])
    return diagonal[None], self_energy[None]


def solution(mesh):
    blocks = P("energy", "seg", None, None, None)
    energies = mesh.shape["energy"]
    nx = math.isqrt(energies)
    return jax.shard_map(
        functools.partial(per_device, energies // nx, nx),
        mesh=mesh,
        in_specs=(blocks, blocks, blocks, P("energy", "seg"), blocks),
        out_specs=(blocks, blocks),
        check_vma=False,
    )
```

```python
import functools
import math

import jax
import jax.numpy as jnp
from jax import lax
from jax.experimental import pallas as pl
from jax.experimental.pallas import tpu as pltpu
from jax.sharding import PartitionSpec as P

F32 = jnp.float32
BF16 = jnp.bfloat16
MESH = pl.DeviceIdType.MESH

G0, X0, Y0 = 3, 10, 17
T0, T1, A_IN, C_IN, RS, RP, RQ, U, W, M_IN, CUR = range(21, 32)
PLACES = 32
BLOCKS = 4


def dft(values):
    n = len(values)
    if n == 1:
        return values
    even, odd = dft(values[0::2]), dft(values[1::2])
    out = [None] * n
    half = n // 2
    for j in range(half):
        er, ei = even[j]
        orr, oi = odd[j]
        angle = -2.0 * math.pi * j / n
        cos, sin = math.cos(angle), math.sin(angle)
        if j == 0:
            tr, ti = orr, oi
        elif 4 * j == n:
            tr, ti = oi, -orr
        elif 8 * j == n:
            tr, ti = (orr + oi) * cos, (oi - orr) * cos
        elif 8 * j == 3 * n:
            tr, ti = (oi - orr) * -cos, (orr + oi) * cos
        else:
            tr, ti = orr * cos - oi * sin, orr * sin + oi * cos
        out[j] = (er + tr, ei + ti)
        out[j + half] = (er - tr, ei - ti)
    return out


def kernel(
    ny, nx,
    g_hbm, a_hbm, c_hbm, m_ref, w_hbm, diag_hbm, self_hbm,
    gf, af, cf, sf, pqf, rx, co, mi, oi, dg, rows, srows, res, ops,
    in_sem, sc_sem, x_send, x_recv, ch_sem, fw_sem, a_send, a_recv, r_send, r_recv, out_sem,
):
    ne = ny * nx
    depth = dg.shape[2] // ne
    width = dg.shape[3]
    seg = lax.axis_index("seg")
    me = lax.axis_index("energy")
    z, c = lax.div(seg, 2), lax.rem(seg, 2)
    nz = lax.axis_size("seg") // 2
    last = nz - 1
    my_y, my_x = lax.div(me, nx), lax.rem(me, nx)
    k = c * z + (1 - c) * (last - z)
    partner = seg + 1 - 2 * c
    onward = seg + 4 * c - 2
    high = lax.div(2 * z, nz)

    def peer(offset):
        dy, dx = lax.div(offset, nx), lax.rem(offset, nx)
        return lax.rem(my_y + dy, ny) * nx + lax.rem(my_x + dx, nx)

    def rows_of(energy):
        return pl.ds(pl.multiple_of(energy * depth, depth), depth)

    def load(b):
        return [
            pltpu.make_async_copy(src.at[b], dst.at[b], in_sem.at[b, j])
            for j, (src, dst) in enumerate(((g_hbm, gf), (a_hbm, af), (c_hbm, cf)))
        ]

    for b in range(BLOCKS):
        for copy in load(b):
            copy.start()

    barrier = pltpu.get_barrier_semaphore()

    @pl.loop(1, ne)
    def _(offset):
        pl.semaphore_signal(barrier, inc=1, device_id=(seg, peer(offset)), device_id_type=MESH)

    pl.semaphore_signal(barrier, inc=1, device_id=(partner, me), device_id_type=MESH)

    @pl.when(z > 0)
    def _():
        pl.semaphore_signal(barrier, inc=1, device_id=(seg - 2, me), device_id_type=MESH)

    @pl.when(z < last)
    def _():
        pl.semaphore_signal(barrier, inc=1, device_id=(seg + 2, me), device_id_type=MESH)

    def split_store(place, real, imag):
        for q, value in enumerate((real, imag, real + imag)):
            top = value.astype(BF16)
            ops[place, q, 0] = top
            ops[place, q, 1] = (value - top.astype(F32)).astype(BF16)

    def product(left, right):
        parts = []
        for q in range(3):
            lhs = jnp.concatenate([ops[left, q, 0], ops[left, q, 0], ops[left, q, 1]], axis=1)
            rhs = jnp.concatenate([ops[right, q, 0], ops[right, q, 1], ops[right, q, 0]], axis=0)
            parts.append(jnp.dot(lhs, rhs, preferred_element_type=F32))
        return parts[0] - parts[1], parts[2] - parts[0] - parts[1]

    dg[...] = jnp.zeros(dg.shape, F32)
    for b in range(BLOCKS):
        for copy in load(b):
            copy.wait()
        weight = m_ref[0, b].astype(F32)
        af[b] = af[b] * weight
        split_store(G0 - b, gf[b, 0], gf[b, 1])
        split_store(A_IN, af[b, 0], af[b, 1])
        split_store(C_IN, cf[b, 0], cf[b, 1])
        split_store(X0 - b, *product(G0 - b, A_IN))
        split_store(Y0 - b, *product(C_IN, G0 - b))

    neighbours = lax.div(z + last, nz) + lax.div(last - z + last, nz)
    pl.semaphore_wait(barrier, ne + neighbours)

    @pl.loop(1, ne)
    def _(offset):
        to = peer(offset)
        pltpu.make_async_remote_copy(
            src_ref=w_hbm.at[:, :, rows_of(to), :],
            dst_ref=srows.at[me],
            send_sem=sc_sem.at[0],
            recv_sem=sc_sem.at[1],
            device_id=(seg, to),
            device_id_type=MESH,
        ).start()

    own_screen = pltpu.make_async_copy(w_hbm.at[:, :, rows_of(me), :], srows.at[me], sc_sem.at[2])
    own_screen.start()

    def exchange(j, src):
        return pltpu.make_async_remote_copy(
            src_ref=src,
            dst_ref=rx.at[j],
            send_sem=x_send.at[j],
            recv_sem=x_recv.at[j],
            device_id=(partner, me),
            device_id_type=MESH,
        )

    swap_source = exchange(0, sf.at[c])
    swap_p, swap_q = exchange(1, pqf.at[0]), exchange(2, pqf.at[1])

    own_p, own_q = X0 + BLOCKS - 1, Y0 + BLOCKS - 1
    own_left = c * own_p + (1 - c) * own_q
    own_right = c * own_q + (1 - c) * own_p
    his_left = RP + 1 - c
    his_right = RP + c
    relay = pltpu.make_async_remote_copy(
        src_ref=co, dst_ref=mi, send_sem=ch_sem.at[0], recv_sem=ch_sem.at[1],
        device_id=(onward, me), device_id_type=MESH,
    )
    forward = pltpu.make_async_remote_copy(
        src_ref=mi, dst_ref=oi, send_sem=fw_sem.at[0], recv_sem=fw_sem.at[1],
        device_id=(partner, me), device_id_type=MESH,
    )

    def chain(direction, outer):
        for b in range(BLOCKS):
            j = BLOCKS - 1 - b
            if direction == 0 and b > 0:
                split_store(T0, *product(X0 - b, G0 + b - 1))
            if direction == 1 and b == 0:
                split_store(T1, af[j, 0], af[j, 1])
            if direction == 1 and b > 0:
                real, imag = product(CUR, X0 - j)
                split_store(T1, real + af[j, 0], imag + af[j, 1])
            if outer and b > 0:
                real, imag = product(X0 - b, X0 + b - 1)
                split_store(X0 + b, real, imag)
                if b == BLOCKS - 1:
                    pqf[0, 0] = real
                    pqf[0, 1] = imag
            if direction == 0 and b > 0:
                real, imag = product(T0, Y0 - b)
                real, imag = real + gf[b, 0], imag + gf[b, 1]
                if b < BLOCKS - 1:
                    split_store(G0 + b, real, imag)
            if direction == 1:
                real, imag = product(Y0 - j, T1)
                if b < BLOCKS - 1:
                    split_store(CUR, real, imag)
            if b == BLOCKS - 1:
                sf[direction, 0] = real
                sf[direction, 1] = imag
            if outer and b > 0:
                real, imag = product(Y0 + b - 1, Y0 - b)
                split_store(Y0 + b, real, imag)
                if b == BLOCKS - 1:
                    pqf[1, 0] = real
                    pqf[1, 1] = imag

        if outer:
            swap_p.start()
            swap_q.start()

        @pl.when(c == direction)
        def _():
            swap_source.start()

    def join():
        swap_source.wait_recv()
        split_store(RS, rx[0, 0], rx[0, 1])
        split_store(T0, *product(own_left, RS))
        real, imag = product(T0, own_right)
        co[0] = real + sf[1 - c, 0]
        co[1] = imag + sf[1 - c, 1]

        @pl.when(k == 0)
        def _():
            relay.start()

    def compose():
        swap_p.wait_recv()
        swap_q.wait_recv()
        split_store(RP, rx[1, 0], rx[1, 1])
        split_store(RQ, rx[2, 0], rx[2, 1])
        split_store(U, *product(own_left, his_left))
        split_store(W, *product(his_right, own_right))

    def batch(b, sem):
        spot = rows.at[b, pl.ds(0, ne - 1)]
        return pltpu.make_async_copy(spot, spot, sem.at[b])

    def diag_out(b):
        return pltpu.make_async_copy(dg.at[b], diag_hbm.at[b], out_sem.at[0, b])

    def publish(second, b, real, imag):
        dg[b, 0] = dg[b, 0] + real
        dg[b, 1] = dg[b, 1] + imag

        @pl.when(second == 1)
        def _():
            @pl.loop(1, ne)
            def _(offset):
                to = peer(offset)
                pltpu.make_async_remote_copy(
                    src_ref=dg.at[b, :, rows_of(to), :],
                    dst_ref=rows.at[b, me],
                    send_sem=a_send.at[b],
                    recv_sem=a_recv.at[b],
                    device_id=(seg, to),
                    device_id_type=MESH,
                ).start()

            diag_out(b).start()
            rows[b, me] = dg[b, :, rows_of(me), :]

    tiles = [(r, v) for r in range(0, depth, 8) for v in range(0, width, 128)]

    def transform_screened():
        spot = srows.at[pl.ds(0, ne - 1)]
        pltpu.make_async_copy(spot, spot, sc_sem.at[1]).wait()
        own_screen.wait()

        @pl.loop(0, BLOCKS)
        def _(b):
            for r, v in tiles:
                at = (pl.ds(r, 8), pl.ds(v, 128))
                values = dft([(srows[(e, b, 0) + at], srows[(e, b, 1) + at]) for e in range(ne)])
                for e in range(ne):
                    srows[(e, b, 0) + at] = values[e][0] * (1.0 / ne)
                    srows[(e, b, 1) + at] = values[e][1] * (1.0 / ne)

    def pass_on():
        relay.wait_recv()
        forward.start()
        split_store(M_IN, mi[0], mi[1])

        @pl.when(k < last)
        def _():
            split_store(T0, *product(U, M_IN))
            real, imag = product(T0, W)
            co[0] = co[0] + real
            co[1] = co[1] + imag
            relay.start()

    def sweep(second, direction):
        own = lax.rem(direction + c, 2) == 1

        @pl.when(own & (k > 0))
        def _():
            split_store(T0, *product(his_left, M_IN))
            real, imag = product(T0, his_right)
            split_store(CUR, real + rx[0, 0], imag + rx[0, 1])

        @pl.when(own & (k == 0))
        def _():
            split_store(CUR, rx[0, 0], rx[0, 1])

        @pl.when(jnp.logical_not(own) & (k < last))
        def _():
            forward.wait_recv()
            split_store(CUR, oi[0], oi[1])

        @pl.when(jnp.logical_not(own) & (k == last))
        def _():
            ops[CUR] = jnp.zeros(ops.shape[1:], BF16)

        @pl.when(direction == 0)
        def _():
            for b in range(BLOCKS):
                split_store(T0, *product(X0 - b, CUR))
                real, imag = product(T0, Y0 - b)
                real, imag = real + gf[b, 0], imag + gf[b, 1]
                if b < BLOCKS - 1:
                    split_store(CUR, real, imag)
                publish(second, b, real, imag)

        @pl.when(direction == 1)
        def _():
            for b in reversed(range(BLOCKS)):
                split_store(T0, *product(G0 - b, CUR))
                if b > 0:
                    real, imag = product(CUR, X0 - b)
                    split_store(T1, real + af[b, 0], imag + af[b, 1])
                publish(second, b, *product(T0, G0 - b))
                if b > 0:
                    split_store(CUR, *product(Y0 - b, T1))

    for i in range(2):
        if i == 1:
            @pl.when(k == 1)
            def _():
                pass_on()

        for side in range(2):
            @pl.when(high == side)
            def _():
                chain((i + side) % 2, i == 0)

        @pl.when(lax.rem(i + high + c, 2) == 1)
        def _():
            join()

        if i == 0:
            compose()

    @pl.loop(2, 4)
    def _(i):
        @pl.when(i == k)
        def _():
            pass_on()

        sweep(i - 2, lax.rem(i + high, 2))

    transform_screened()

    def own_self(b):
        return pltpu.make_async_copy(
            res.at[b, me], self_hbm.at[b, :, rows_of(me), :], out_sem.at[1, b]
        )

    @pl.loop(0, BLOCKS)
    def _(j):
        b = high * j + (1 - high) * (BLOCKS - 1 - j)
        batch(b, a_recv).wait()
        for r, v in tiles:
            at = (pl.ds(r, 8), pl.ds(v, 128))
            values = dft([(rows[(b, e, 0) + at], rows[(b, e, 1) + at]) for e in range(ne)])
            mixed = []
            for e in range(ne):
                vr, vi = values[e]
                wr, wi = srows[(e, b, 0) + at], srows[(e, b, 1) + at]
                mixed.append((vr * wi + vi * wr, vr * wr - vi * wi))
            values = dft(mixed)
            for e in range(ne):
                res[(b, e, 0) + at] = values[e][1]
                res[(b, e, 1) + at] = values[e][0]

        @pl.loop(1, ne)
        def _(offset):
            to = peer(offset)
            pltpu.make_async_remote_copy(
                src_ref=res.at[b, to],
                dst_ref=self_hbm.at[b, :, rows_of(me), :],
                send_sem=r_send.at[b],
                recv_sem=r_recv.at[b],
                device_id=(seg, to),
                device_id_type=MESH,
            ).start()

        own_self(b).start()

    @pl.loop(0, BLOCKS)
    def _(b):
        for sem in (a_send, r_send, r_recv):
            batch(b, sem).wait()
        diag_out(b).wait()
        own_self(b).wait()

    spot = srows.at[pl.ds(0, ne - 1)]
    pltpu.make_async_copy(spot, spot, sc_sem.at[0]).wait()
    swap_source.wait_send()
    swap_p.wait_send()
    swap_q.wait_send()

    @pl.when(k < last)
    def _():
        relay.wait_send()

    @pl.when(k > 0)
    def _():
        forward.wait_send()


def hand_over(diag_in, self_in, diag_hbm, self_hbm, sem):
    copies = [
        pltpu.make_async_copy(src.at[b], dst.at[b], sem.at[j, b])
        for b in range(BLOCKS)
        for j, (src, dst) in enumerate(((diag_in, diag_hbm), (self_in, self_hbm)))
    ]
    for copy in copies:
        copy.start()
    for copy in copies:
        copy.wait()


def per_device(ny, nx, green, couple_left, couple_right, coupling, screened):
    shape = green.shape[1:]
    blocks, _, order, _ = shape
    ne = ny * nx
    depth = order // ne
    one = (2, order, order)
    anywhere = pl.BlockSpec(memory_space=pl.ANY)
    diagonal, self_energy = pl.pallas_call(
        functools.partial(kernel, ny, nx),
        out_shape=[jax.ShapeDtypeStruct(shape, F32)] * 2,
        in_specs=[anywhere] * 3 + [pl.BlockSpec(memory_space=pltpu.SMEM), anywhere],
        out_specs=[anywhere] * 2,
        scratch_shapes=[
            pltpu.VMEM(shape, F32),
            pltpu.VMEM(shape, F32),
            pltpu.VMEM(shape, F32),
            pltpu.VMEM((2,) + one, F32),
            pltpu.VMEM((2,) + one, F32),
            pltpu.VMEM((3,) + one, F32),
            pltpu.VMEM(one, F32),
            pltpu.VMEM(one, F32),
            pltpu.VMEM(one, F32),
            pltpu.VMEM(shape, F32),
            pltpu.VMEM((blocks, ne, 2, depth, order), F32),
            pltpu.VMEM((ne, blocks, 2, depth, order), F32),
            pltpu.VMEM((blocks, ne, 2, depth, order), F32),
            pltpu.VMEM((PLACES, 3, 2, order, order), BF16),
            pltpu.SemaphoreType.DMA((blocks, 3)),
            pltpu.SemaphoreType.DMA((3,)),
            pltpu.SemaphoreType.DMA((3,)),
            pltpu.SemaphoreType.DMA((3,)),
            pltpu.SemaphoreType.DMA((2,)),
            pltpu.SemaphoreType.DMA((2,)),
            pltpu.SemaphoreType.DMA((blocks,)),
            pltpu.SemaphoreType.DMA((blocks,)),
            pltpu.SemaphoreType.DMA((blocks,)),
            pltpu.SemaphoreType.DMA((blocks,)),
            pltpu.SemaphoreType.DMA((2, blocks)),
        ],
        compiler_params=pltpu.CompilerParams(
            collective_id=0, has_side_effects=True, vmem_limit_bytes=48 * 2**20
        ),
    )(green[0], couple_left[0], couple_right[0], coupling, screened[0])
    diagonal, self_energy = pl.pallas_call(
        hand_over,
        out_shape=[jax.ShapeDtypeStruct(shape, F32)] * 2,
        in_specs=[anywhere] * 2,
        out_specs=[anywhere] * 2,
        scratch_shapes=[pltpu.SemaphoreType.DMA((2, blocks))],
        compiler_params=pltpu.CompilerParams(vmem_limit_bytes=2**21),
    )(diagonal, self_energy)
    return diagonal[None], self_energy[None]


def solution(mesh):
    blocks = P("energy", "seg", None, None, None)
    energies = mesh.shape["energy"]
    nx = math.isqrt(energies)
    return jax.shard_map(
        functools.partial(per_device, energies // nx, nx),
        mesh=mesh,
        in_specs=(blocks, blocks, blocks, P("energy", "seg"), blocks),
        out_specs=(blocks, blocks),
        check_vma=False,
    )
```

```python
import functools
import math

import jax
import jax.numpy as jnp
from jax import lax
from jax.experimental import pallas as pl
from jax.experimental.pallas import tpu as pltpu
from jax.sharding import PartitionSpec as P

F32 = jnp.float32
BF16 = jnp.bfloat16
MESH = pl.DeviceIdType.MESH

G0, X0, Y0 = 3, 10, 17
T0, T1, A_IN, C_IN, RS, RP, RQ, U, W, M_IN, CUR = range(21, 32)
PLACES = 32
BLOCKS = 4


def dft(values):
    n = len(values)
    if n == 1:
        return values
    even, odd = dft(values[0::2]), dft(values[1::2])
    out = [None] * n
    half = n // 2
    for j in range(half):
        er, ei = even[j]
        orr, oi = odd[j]
        angle = -2.0 * math.pi * j / n
        cos, sin = math.cos(angle), math.sin(angle)
        if j == 0:
            tr, ti = orr, oi
        elif 4 * j == n:
            tr, ti = oi, -orr
        elif 8 * j == n:
            tr, ti = (orr + oi) * cos, (oi - orr) * cos
        elif 8 * j == 3 * n:
            tr, ti = (oi - orr) * -cos, (orr + oi) * cos
        else:
            tr, ti = orr * cos - oi * sin, orr * sin + oi * cos
        out[j] = (er + tr, ei + ti)
        out[j + half] = (er - tr, ei - ti)
    return out


def kernel(
    ny, nx,
    g_hbm, a_hbm, c_hbm, m_ref, w_hbm, diag_hbm, self_hbm,
    gf, af, cf, sf, pqf, rx, co, mi, oi, dg, rows, srows, res, ops,
    in_sem, sc_sem, x_send, x_recv, ch_sem, fw_sem, a_send, a_recv, r_send, r_recv, out_sem,
):
    ne = ny * nx
    depth = dg.shape[2] // ne
    width = dg.shape[3]
    seg = lax.axis_index("seg")
    me = lax.axis_index("energy")
    z, c = lax.div(seg, 2), lax.rem(seg, 2)
    nz = lax.axis_size("seg") // 2
    last = nz - 1
    my_y, my_x = lax.div(me, nx), lax.rem(me, nx)
    k = c * z + (1 - c) * (last - z)
    partner = seg + 1 - 2 * c
    onward = seg + 4 * c - 2
    high = lax.div(2 * z, nz)

    def peer(offset):
        dy, dx = lax.div(offset, nx), lax.rem(offset, nx)
        return lax.rem(my_y + dy, ny) * nx + lax.rem(my_x + dx, nx)

    def rows_of(energy):
        return pl.ds(pl.multiple_of(energy * depth, depth), depth)

    def load(b):
        return [
            pltpu.make_async_copy(src.at[b], dst.at[b], in_sem.at[b, j])
            for j, (src, dst) in enumerate(((g_hbm, gf), (a_hbm, af), (c_hbm, cf)))
        ]

    for b in range(BLOCKS):
        for copy in load(b):
            copy.start()

    barrier = pltpu.get_barrier_semaphore()

    @pl.loop(1, ne)
    def _(offset):
        pl.semaphore_signal(barrier, inc=1, device_id=(seg, peer(offset)), device_id_type=MESH)

    pl.semaphore_signal(barrier, inc=1, device_id=(partner, me), device_id_type=MESH)

    @pl.when(z > 0)
    def _():
        pl.semaphore_signal(barrier, inc=1, device_id=(seg - 2, me), device_id_type=MESH)

    @pl.when(z < last)
    def _():
        pl.semaphore_signal(barrier, inc=1, device_id=(seg + 2, me), device_id_type=MESH)

    def split_store(place, real, imag, rows_in=slice(None)):
        for q, value in enumerate((real, imag, real + imag)):
            top = value.astype(BF16)
            ops[place, q, 0, rows_in] = top
            ops[place, q, 1, rows_in] = (value - top.astype(F32)).astype(BF16)

    def product(left, right, rows_in=slice(None), inner=slice(None)):
        parts = []
        for q in range(3):
            lhs = [ops[left, q, part, rows_in, inner] for part in (0, 0, 1)]
            rhs = [ops[right, q, part, inner] for part in (0, 1, 0)]
            parts.append(
                jnp.dot(
                    jnp.concatenate(lhs, axis=1),
                    jnp.concatenate(rhs, axis=0),
                    preferred_element_type=F32,
                )
            )
        return parts[0] - parts[1], parts[2] - parts[0] - parts[1]

    dg[...] = jnp.zeros(dg.shape, F32)
    for b in range(BLOCKS):
        for copy in load(b):
            copy.wait()
        weight = m_ref[0, b].astype(F32)
        af[b] = af[b] * weight
        split_store(G0 - b, gf[b, 0], gf[b, 1])
        split_store(A_IN, af[b, 0], af[b, 1])
        split_store(C_IN, cf[b, 0], cf[b, 1])
        split_store(X0 - b, *product(G0 - b, A_IN))
        split_store(Y0 - b, *product(C_IN, G0 - b))

    neighbours = lax.div(z + last, nz) + lax.div(last - z + last, nz)
    pl.semaphore_wait(barrier, ne + neighbours)

    @pl.loop(1, ne)
    def _(offset):
        to = peer(offset)
        pltpu.make_async_remote_copy(
            src_ref=w_hbm.at[:, :, rows_of(to), :],
            dst_ref=srows.at[me],
            send_sem=sc_sem.at[0],
            recv_sem=sc_sem.at[1],
            device_id=(seg, to),
            device_id_type=MESH,
        ).start()

    own_screen = pltpu.make_async_copy(w_hbm.at[:, :, rows_of(me), :], srows.at[me], sc_sem.at[2])
    own_screen.start()

    def exchange(j, src):
        return pltpu.make_async_remote_copy(
            src_ref=src,
            dst_ref=rx.at[j],
            send_sem=x_send.at[j],
            recv_sem=x_recv.at[j],
            device_id=(partner, me),
            device_id_type=MESH,
        )

    swap_source = exchange(0, sf.at[c])
    swap_p, swap_q = exchange(1, pqf.at[0]), exchange(2, pqf.at[1])

    own_p, own_q = X0 + BLOCKS - 1, Y0 + BLOCKS - 1
    own_left = c * own_p + (1 - c) * own_q
    own_right = c * own_q + (1 - c) * own_p
    his_left = RP + 1 - c
    his_right = RP + c
    order = dg.shape[2]
    halves = [slice(h * order // 2, (h + 1) * order // 2) for h in range(2)]
    relay = [
        pltpu.make_async_remote_copy(
            src_ref=co.at[:, half], dst_ref=mi.at[:, half],
            send_sem=ch_sem.at[0, h], recv_sem=ch_sem.at[1, h],
            device_id=(onward, me), device_id_type=MESH,
        )
        for h, half in enumerate(halves)
    ]
    forward = [
        pltpu.make_async_remote_copy(
            src_ref=mi.at[:, half], dst_ref=oi.at[:, half],
            send_sem=fw_sem.at[0, h], recv_sem=fw_sem.at[1, h],
            device_id=(partner, me), device_id_type=MESH,
        )
        for h, half in enumerate(halves)
    ]

    def chain(direction, outer):
        for b in range(BLOCKS):
            j = BLOCKS - 1 - b
            if direction == 0 and b > 0:
                split_store(T0, *product(X0 - b, G0 + b - 1))
            if direction == 1 and b == 0:
                split_store(T1, af[j, 0], af[j, 1])
            if direction == 1 and b > 0:
                real, imag = product(CUR, X0 - j)
                split_store(T1, real + af[j, 0], imag + af[j, 1])
            if outer and b > 0:
                real, imag = product(X0 - b, X0 + b - 1)
                split_store(X0 + b, real, imag)
                if b == BLOCKS - 1:
                    pqf[0, 0] = real
                    pqf[0, 1] = imag
            if direction == 0 and b > 0:
                real, imag = product(T0, Y0 - b)
                real, imag = real + gf[b, 0], imag + gf[b, 1]
                if b < BLOCKS - 1:
                    split_store(G0 + b, real, imag)
            if direction == 1:
                real, imag = product(Y0 - j, T1)
                if b < BLOCKS - 1:
                    split_store(CUR, real, imag)
            if b == BLOCKS - 1:
                sf[direction, 0] = real
                sf[direction, 1] = imag
            if outer and b > 0:
                real, imag = product(Y0 + b - 1, Y0 - b)
                split_store(Y0 + b, real, imag)
                if b == BLOCKS - 1:
                    pqf[1, 0] = real
                    pqf[1, 1] = imag

        if outer:
            swap_p.start()
            swap_q.start()

        @pl.when(c == direction)
        def _():
            swap_source.start()

    def join():
        swap_source.wait_recv()
        split_store(RS, rx[0, 0], rx[0, 1])
        split_store(T0, *product(own_left, RS))
        for h, half in enumerate(halves):
            real, imag = product(T0, own_right, half)
            co[0, half] = real + sf[1 - c, 0, half]
            co[1, half] = imag + sf[1 - c, 1, half]

            @pl.when(k == 0)
            def _():
                relay[h].start()

    def compose():
        swap_p.wait_recv()
        swap_q.wait_recv()
        split_store(RP, rx[1, 0], rx[1, 1])
        split_store(RQ, rx[2, 0], rx[2, 1])

        @pl.when(k < last)
        def _():
            split_store(U, *product(own_left, his_left))
            split_store(W, *product(his_right, own_right))

        @pl.when(k == last)
        def _():
            ops[U] = ops[his_left]
            ops[W] = ops[his_right]

    def batch(b, sem):
        spot = rows.at[b, pl.ds(0, ne - 1)]
        return pltpu.make_async_copy(spot, spot, sem.at[b])

    def diag_out(b):
        return pltpu.make_async_copy(dg.at[b], diag_hbm.at[b], out_sem.at[0, b])

    def publish(second, b, real, imag):
        dg[b, 0] = dg[b, 0] + real
        dg[b, 1] = dg[b, 1] + imag

        @pl.when(second == 1)
        def _():
            @pl.loop(1, ne)
            def _(offset):
                to = peer(offset)
                pltpu.make_async_remote_copy(
                    src_ref=dg.at[b, :, rows_of(to), :],
                    dst_ref=rows.at[b, me],
                    send_sem=a_send.at[b],
                    recv_sem=a_recv.at[b],
                    device_id=(seg, to),
                    device_id_type=MESH,
                ).start()

            diag_out(b).start()
            rows[b, me] = dg[b, :, rows_of(me), :]

    tiles = [(r, v) for r in range(0, depth, 8) for v in range(0, width, 128)]

    def transform_screened():
        spot = srows.at[pl.ds(0, ne - 1)]
        pltpu.make_async_copy(spot, spot, sc_sem.at[1]).wait()
        own_screen.wait()

        @pl.loop(0, BLOCKS)
        def _(b):
            for r, v in tiles:
                at = (pl.ds(r, 8), pl.ds(v, 128))
                values = dft([(srows[(e, b, 0) + at], srows[(e, b, 1) + at]) for e in range(ne)])
                for e in range(ne):
                    srows[(e, b, 0) + at] = values[e][0] * (1.0 / ne)
                    srows[(e, b, 1) + at] = values[e][1] * (1.0 / ne)

    def pass_on():
        @pl.when(k == last)
        def _():
            co[...] = rx[0]

        for h, half in enumerate(halves):
            relay[h].wait_recv()
            forward[h].start()
            split_store(M_IN, mi[0, half], mi[1, half], half)
            split_store(T0, *product(M_IN, W, half), half)
            for g, other in enumerate(halves):
                real, imag = product(U, T0, other, half)
                co[0, other] = co[0, other] + real
                co[1, other] = co[1, other] + imag
                if h == 1:
                    @pl.when(k < last)
                    def _():
                        relay[g].start()

    def sweep(second, direction):
        own = lax.rem(direction + c, 2) == 1

        @pl.when(own & (k == last))
        def _():
            split_store(CUR, co[0], co[1])

        @pl.when(own & (k > 0) & (k < last))
        def _():
            split_store(T0, *product(his_left, M_IN))
            real, imag = product(T0, his_right)
            split_store(CUR, real + rx[0, 0], imag + rx[0, 1])

        @pl.when(own & (k == 0))
        def _():
            split_store(CUR, rx[0, 0], rx[0, 1])

        @pl.when(jnp.logical_not(own) & (k < last))
        def _():
            for half in forward:
                half.wait_recv()
            split_store(CUR, oi[0], oi[1])

        @pl.when(jnp.logical_not(own) & (k == last))
        def _():
            ops[CUR] = jnp.zeros(ops.shape[1:], BF16)

        @pl.when(direction == 0)
        def _():
            for b in range(BLOCKS):
                split_store(T0, *product(X0 - b, CUR))
                real, imag = product(T0, Y0 - b)
                real, imag = real + gf[b, 0], imag + gf[b, 1]
                if b < BLOCKS - 1:
                    split_store(CUR, real, imag)
                publish(second, b, real, imag)

        @pl.when(direction == 1)
        def _():
            for b in reversed(range(BLOCKS)):
                split_store(T0, *product(G0 - b, CUR))
                if b > 0:
                    real, imag = product(CUR, X0 - b)
                    split_store(T1, real + af[b, 0], imag + af[b, 1])
                publish(second, b, *product(T0, G0 - b))
                if b > 0:
                    split_store(CUR, *product(Y0 - b, T1))

    for i in range(2):
        for side in range(2):
            @pl.when(high == side)
            def _():
                chain((i + side) % 2, i == 0)

        if i == 1:
            @pl.when(k == 1)
            def _():
                pass_on()

        @pl.when(lax.rem(i + high + c, 2) == 1)
        def _():
            join()

        if i == 0:
            compose()

    @pl.loop(2, 4)
    def _(i):
        @pl.when(i == k)
        def _():
            pass_on()

        sweep(i - 2, lax.rem(i + high, 2))

    transform_screened()

    def own_self(b):
        return pltpu.make_async_copy(
            res.at[b, me], self_hbm.at[b, :, rows_of(me), :], out_sem.at[1, b]
        )

    @pl.loop(0, BLOCKS)
    def _(j):
        b = high * j + (1 - high) * (BLOCKS - 1 - j)
        batch(b, a_recv).wait()
        for r, v in tiles:
            at = (pl.ds(r, 8), pl.ds(v, 128))
            values = dft([(rows[(b, e, 0) + at], rows[(b, e, 1) + at]) for e in range(ne)])
            mixed = []
            for e in range(ne):
                vr, vi = values[e]
                wr, wi = srows[(e, b, 0) + at], srows[(e, b, 1) + at]
                mixed.append((vr * wi + vi * wr, vr * wr - vi * wi))
            values = dft(mixed)
            for e in range(ne):
                res[(b, e, 0) + at] = values[e][1]
                res[(b, e, 1) + at] = values[e][0]

        @pl.loop(1, ne)
        def _(offset):
            to = peer(offset)
            pltpu.make_async_remote_copy(
                src_ref=res.at[b, to],
                dst_ref=self_hbm.at[b, :, rows_of(me), :],
                send_sem=r_send.at[b],
                recv_sem=r_recv.at[b],
                device_id=(seg, to),
                device_id_type=MESH,
            ).start()

        own_self(b).start()

    @pl.loop(0, BLOCKS)
    def _(b):
        for sem in (a_send, r_send, r_recv):
            batch(b, sem).wait()
        diag_out(b).wait()
        own_self(b).wait()

    spot = srows.at[pl.ds(0, ne - 1)]
    pltpu.make_async_copy(spot, spot, sc_sem.at[0]).wait()
    swap_source.wait_send()
    swap_p.wait_send()
    swap_q.wait_send()

    @pl.when(k < last)
    def _():
        for half in relay:
            half.wait_send()

    @pl.when(k > 0)
    def _():
        for half in forward:
            half.wait_send()


def hand_over(diag_in, self_in, diag_hbm, self_hbm, sem):
    copies = [
        pltpu.make_async_copy(src.at[b], dst.at[b], sem.at[j, b])
        for b in range(BLOCKS)
        for j, (src, dst) in enumerate(((diag_in, diag_hbm), (self_in, self_hbm)))
    ]
    for copy in copies:
        copy.start()
    for copy in copies:
        copy.wait()


def per_device(ny, nx, green, couple_left, couple_right, coupling, screened):
    shape = green.shape[1:]
    blocks, _, order, _ = shape
    ne = ny * nx
    depth = order // ne
    one = (2, order, order)
    anywhere = pl.BlockSpec(memory_space=pl.ANY)
    diagonal, self_energy = pl.pallas_call(
        functools.partial(kernel, ny, nx),
        out_shape=[jax.ShapeDtypeStruct(shape, F32)] * 2,
        in_specs=[anywhere] * 3 + [pl.BlockSpec(memory_space=pltpu.SMEM), anywhere],
        out_specs=[anywhere] * 2,
        scratch_shapes=[
            pltpu.VMEM(shape, F32),
            pltpu.VMEM(shape, F32),
            pltpu.VMEM(shape, F32),
            pltpu.VMEM((2,) + one, F32),
            pltpu.VMEM((2,) + one, F32),
            pltpu.VMEM((3,) + one, F32),
            pltpu.VMEM(one, F32),
            pltpu.VMEM(one, F32),
            pltpu.VMEM(one, F32),
            pltpu.VMEM(shape, F32),
            pltpu.VMEM((blocks, ne, 2, depth, order), F32),
            pltpu.VMEM((ne, blocks, 2, depth, order), F32),
            pltpu.VMEM((blocks, ne, 2, depth, order), F32),
            pltpu.VMEM((PLACES, 3, 2, order, order), BF16),
            pltpu.SemaphoreType.DMA((blocks, 3)),
            pltpu.SemaphoreType.DMA((3,)),
            pltpu.SemaphoreType.DMA((3,)),
            pltpu.SemaphoreType.DMA((3,)),
            pltpu.SemaphoreType.DMA((2, 2)),
            pltpu.SemaphoreType.DMA((2, 2)),
            pltpu.SemaphoreType.DMA((blocks,)),
            pltpu.SemaphoreType.DMA((blocks,)),
            pltpu.SemaphoreType.DMA((blocks,)),
            pltpu.SemaphoreType.DMA((blocks,)),
            pltpu.SemaphoreType.DMA((2, blocks)),
        ],
        compiler_params=pltpu.CompilerParams(
            collective_id=0, has_side_effects=True, vmem_limit_bytes=48 * 2**20
        ),
    )(green[0], couple_left[0], couple_right[0], coupling, screened[0])
    diagonal, self_energy = pl.pallas_call(
        hand_over,
        out_shape=[jax.ShapeDtypeStruct(shape, F32)] * 2,
        in_specs=[anywhere] * 2,
        out_specs=[anywhere] * 2,
        scratch_shapes=[pltpu.SemaphoreType.DMA((2, blocks))],
        compiler_params=pltpu.CompilerParams(vmem_limit_bytes=2**21),
    )(diagonal, self_energy)
    return diagonal[None], self_energy[None]


def solution(mesh):
    blocks = P("energy", "seg", None, None, None)
    energies = mesh.shape["energy"]
    nx = math.isqrt(energies)
    return jax.shard_map(
        functools.partial(per_device, energies // nx, nx),
        mesh=mesh,
        in_specs=(blocks, blocks, blocks, P("energy", "seg"), blocks),
        out_specs=(blocks, blocks),
        check_vma=False,
    )
```

```python
import functools
import math

import jax
import jax.numpy as jnp
from jax import lax
from jax.experimental import pallas as pl
from jax.experimental.pallas import tpu as pltpu
from jax.sharding import PartitionSpec as P

F32 = jnp.float32
BF16 = jnp.bfloat16
MESH = pl.DeviceIdType.MESH

G0, X0, Y0 = 3, 10, 17
T0, T1, A_IN, C_IN, RS, RP, RQ, U, W, M_IN, CUR = range(21, 32)
PLACES = 32
BLOCKS = 4


def dft(values):
    n = len(values)
    if n == 1:
        return values
    even, odd = dft(values[0::2]), dft(values[1::2])
    out = [None] * n
    half = n // 2
    for j in range(half):
        er, ei = even[j]
        orr, oi = odd[j]
        angle = -2.0 * math.pi * j / n
        cos, sin = math.cos(angle), math.sin(angle)
        if j == 0:
            tr, ti = orr, oi
        elif 4 * j == n:
            tr, ti = oi, -orr
        elif 8 * j == n:
            tr, ti = (orr + oi) * cos, (oi - orr) * cos
        elif 8 * j == 3 * n:
            tr, ti = (oi - orr) * -cos, (orr + oi) * cos
        else:
            tr, ti = orr * cos - oi * sin, orr * sin + oi * cos
        out[j] = (er + tr, ei + ti)
        out[j + half] = (er - tr, ei - ti)
    return out


def kernel(
    ny, nx,
    g_hbm, a_hbm, c_hbm, m_ref, w_hbm, diag_hbm, self_hbm,
    gf, af, cf, sf, pqf, rx, co, mi, oi, dg, rows, srows, res, ops,
    in_sem, sc_sem, x_send, x_recv, ch_sem, fw_sem, a_send, a_recv, r_send, r_recv, out_sem,
):
    ne = ny * nx
    depth = dg.shape[2] // ne
    width = dg.shape[3]
    seg = lax.axis_index("seg")
    me = lax.axis_index("energy")
    z, c = lax.div(seg, 2), lax.rem(seg, 2)
    nz = lax.axis_size("seg") // 2
    last = nz - 1
    my_y, my_x = lax.div(me, nx), lax.rem(me, nx)
    k = c * z + (1 - c) * (last - z)
    partner = seg + 1 - 2 * c
    onward = seg + 4 * c - 2
    high = lax.div(2 * z, nz)

    def stride(j, n):
        return lax.rem(2 - j + 3 * lax.div(j, 2) - 2 * lax.div(j, 3), 4) if n == 4 else n - 1 - j

    def peer(turn):
        dy, dx = stride(lax.div(turn, nx), ny), stride(lax.rem(turn, nx), nx)
        return lax.rem(my_y + dy, ny) * nx + lax.rem(my_x + dx, nx)

    def rows_of(energy):
        return pl.ds(pl.multiple_of(energy * depth, depth), depth)

    def load(b):
        return [
            pltpu.make_async_copy(src.at[b], dst.at[b], in_sem.at[b, j])
            for j, (src, dst) in enumerate(((g_hbm, gf), (a_hbm, af), (c_hbm, cf)))
        ]

    for b in range(BLOCKS):
        for copy in load(b):
            copy.start()

    barrier = pltpu.get_barrier_semaphore()

    pl.semaphore_signal(barrier, inc=1, device_id=(partner, me), device_id_type=MESH)

    @pl.when(z > 0)
    def _():
        pl.semaphore_signal(barrier, inc=1, device_id=(seg - 2, me), device_id_type=MESH)

    @pl.when(z < last)
    def _():
        pl.semaphore_signal(barrier, inc=1, device_id=(seg + 2, me), device_id_type=MESH)

    def split_store(place, real, imag, rows_in=slice(None)):
        for q, value in enumerate((real, imag, real + imag)):
            top = value.astype(BF16)
            ops[place, q, 0, rows_in] = top
            ops[place, q, 1, rows_in] = (value - top.astype(F32)).astype(BF16)

    def product(left, right, rows_in=slice(None), inner=slice(None)):
        parts = []
        for q in range(3):
            lhs = [ops[left, q, part, rows_in, inner] for part in (0, 0, 1)]
            rhs = [ops[right, q, part, inner] for part in (0, 1, 0)]
            parts.append(
                jnp.dot(
                    jnp.concatenate(lhs, axis=1),
                    jnp.concatenate(rhs, axis=0),
                    preferred_element_type=F32,
                )
            )
        return parts[0] - parts[1], parts[2] - parts[0] - parts[1]

    dg[...] = jnp.zeros(dg.shape, F32)
    for b in range(BLOCKS):
        for copy in load(b):
            copy.wait()
        weight = m_ref[0, b].astype(F32)
        af[b] = af[b] * weight
        split_store(G0 - b, gf[b, 0], gf[b, 1])
        split_store(A_IN, af[b, 0], af[b, 1])
        split_store(C_IN, cf[b, 0], cf[b, 1])
        for energy in range(b * (ne - 1) // BLOCKS, (b + 1) * (ne - 1) // BLOCKS):
            other = lax.rem(me + 1 + energy, ne)
            pl.semaphore_signal(barrier, inc=1, device_id=(seg, other), device_id_type=MESH)
        split_store(X0 - b, *product(G0 - b, A_IN))
        split_store(Y0 - b, *product(C_IN, G0 - b))

    neighbours = lax.div(z + last, nz) + lax.div(last - z + last, nz)
    own_screen = pltpu.make_async_copy(w_hbm.at[:, :, rows_of(me), :], srows.at[me], sc_sem.at[2])
    own_screen.start()

    def send_screened():
        @pl.loop(0, ne - 1)
        def _(turn):
            to = peer(turn)
            pltpu.make_async_remote_copy(
                src_ref=w_hbm.at[:, :, rows_of(to), :],
                dst_ref=srows.at[me],
                send_sem=sc_sem.at[0],
                recv_sem=sc_sem.at[1],
                device_id=(seg, to),
                device_id_type=MESH,
            ).start()

    def exchange(j, src):
        return pltpu.make_async_remote_copy(
            src_ref=src,
            dst_ref=rx.at[j],
            send_sem=x_send.at[j],
            recv_sem=x_recv.at[j],
            device_id=(partner, me),
            device_id_type=MESH,
        )

    swap_source = exchange(0, sf.at[c])
    swap_p, swap_q = exchange(1, pqf.at[0]), exchange(2, pqf.at[1])

    own_p, own_q = X0 + BLOCKS - 1, Y0 + BLOCKS - 1
    own_left = c * own_p + (1 - c) * own_q
    own_right = c * own_q + (1 - c) * own_p
    his_left = RP + 1 - c
    his_right = RP + c
    order = dg.shape[2]
    halves = [slice(h * order // 2, (h + 1) * order // 2) for h in range(2)]
    relay = [
        pltpu.make_async_remote_copy(
            src_ref=co.at[:, half], dst_ref=mi.at[:, half],
            send_sem=ch_sem.at[0, h], recv_sem=ch_sem.at[1, h],
            device_id=(onward, me), device_id_type=MESH,
        )
        for h, half in enumerate(halves)
    ]
    forward = [
        pltpu.make_async_remote_copy(
            src_ref=mi.at[:, half], dst_ref=oi.at[:, half],
            send_sem=fw_sem.at[0, h], recv_sem=fw_sem.at[1, h],
            device_id=(partner, me), device_id_type=MESH,
        )
        for h, half in enumerate(halves)
    ]

    def chain(direction, outer):
        for b in range(BLOCKS):
            j = BLOCKS - 1 - b
            if direction == 0 and b > 0:
                split_store(T0, *product(X0 - b, G0 + b - 1))
            if direction == 1 and b == 0:
                split_store(T1, af[j, 0], af[j, 1])
            if direction == 1 and b > 0:
                real, imag = product(CUR, X0 - j)
                split_store(T1, real + af[j, 0], imag + af[j, 1])
            if outer and b > 0:
                real, imag = product(X0 - b, X0 + b - 1)
                split_store(X0 + b, real, imag)
                if b == BLOCKS - 1:
                    pqf[0, 0] = real
                    pqf[0, 1] = imag
            if direction == 0 and b > 0:
                real, imag = product(T0, Y0 - b)
                real, imag = real + gf[b, 0], imag + gf[b, 1]
                if b < BLOCKS - 1:
                    split_store(G0 + b, real, imag)
            if direction == 1:
                real, imag = product(Y0 - j, T1)
                if b < BLOCKS - 1:
                    split_store(CUR, real, imag)
            if b == BLOCKS - 1:
                sf[direction, 0] = real
                sf[direction, 1] = imag
            if outer and b > 0:
                real, imag = product(Y0 + b - 1, Y0 - b)
                split_store(Y0 + b, real, imag)
                if b == BLOCKS - 1:
                    pqf[1, 0] = real
                    pqf[1, 1] = imag

    def join():
        swap_source.wait_recv()
        split_store(RS, rx[0, 0], rx[0, 1])
        split_store(T0, *product(own_left, RS))
        for h, half in enumerate(halves):
            real, imag = product(T0, own_right, half)
            co[0, half] = real + sf[1 - c, 0, half]
            co[1, half] = imag + sf[1 - c, 1, half]

            @pl.when(k == 0)
            def _():
                relay[h].start()

    def compose():
        swap_p.wait_recv()
        swap_q.wait_recv()
        split_store(RP, rx[1, 0], rx[1, 1])
        split_store(RQ, rx[2, 0], rx[2, 1])

        @pl.when(k < last)
        def _():
            split_store(U, *product(own_left, his_left))
            split_store(W, *product(his_right, own_right))

        @pl.when(k == last)
        def _():
            ops[U] = ops[his_left]
            ops[W] = ops[his_right]

    def batch(b, sem):
        spot = rows.at[b, pl.ds(0, ne - 1)]
        return pltpu.make_async_copy(spot, spot, sem.at[b])

    def diag_out(b):
        return pltpu.make_async_copy(dg.at[b], diag_hbm.at[b], out_sem.at[0, b])

    def publish(second, b, real, imag):
        dg[b, 0] = dg[b, 0] + real
        dg[b, 1] = dg[b, 1] + imag

        @pl.when(second == 1)
        def _():
            @pl.loop(0, ne - 1)
            def _(turn):
                to = peer(turn)
                pltpu.make_async_remote_copy(
                    src_ref=dg.at[b, :, rows_of(to), :],
                    dst_ref=rows.at[b, me],
                    send_sem=a_send.at[b],
                    recv_sem=a_recv.at[b],
                    device_id=(seg, to),
                    device_id_type=MESH,
                ).start()

            diag_out(b).start()
            rows[b, me] = dg[b, :, rows_of(me), :]

    tiles = [(r, v) for r in range(0, depth, 8) for v in range(0, width, 128)]

    def transform_screened():
        spot = srows.at[pl.ds(0, ne - 1)]
        pltpu.make_async_copy(spot, spot, sc_sem.at[1]).wait()
        own_screen.wait()

        @pl.loop(0, BLOCKS)
        def _(b):
            for r, v in tiles:
                at = (pl.ds(r, 8), pl.ds(v, 128))
                values = dft([(srows[(e, b, 0) + at], srows[(e, b, 1) + at]) for e in range(ne)])
                for e in range(ne):
                    srows[(e, b, 0) + at] = values[e][0] * (1.0 / ne)
                    srows[(e, b, 1) + at] = values[e][1] * (1.0 / ne)

    def pass_on():
        @pl.when(k == last)
        def _():
            co[...] = rx[0]

        for h, half in enumerate(halves):
            relay[h].wait_recv()
            forward[h].start()
            split_store(M_IN, mi[0, half], mi[1, half], half)
            split_store(T0, *product(M_IN, W, half), half)
            for g, other in enumerate(halves):
                real, imag = product(U, T0, other, half)
                co[0, other] = co[0, other] + real
                co[1, other] = co[1, other] + imag
                if h == 1:
                    @pl.when(k < last)
                    def _():
                        relay[g].start()

    def sweep(second, direction):
        own = lax.rem(direction + c, 2) == 1

        @pl.when(own & (k == last))
        def _():
            split_store(CUR, co[0], co[1])

        @pl.when(own & (k > 0) & (k < last))
        def _():
            split_store(T0, *product(his_left, M_IN))
            real, imag = product(T0, his_right)
            split_store(CUR, real + rx[0, 0], imag + rx[0, 1])

        @pl.when(own & (k == 0))
        def _():
            split_store(CUR, rx[0, 0], rx[0, 1])

        @pl.when(jnp.logical_not(own) & (k < last))
        def _():
            for half in forward:
                half.wait_recv()
            split_store(CUR, oi[0], oi[1])

        @pl.when(jnp.logical_not(own) & (k == last))
        def _():
            ops[CUR] = jnp.zeros(ops.shape[1:], BF16)

        @pl.when(direction == 0)
        def _():
            for b in range(BLOCKS):
                split_store(T0, *product(X0 - b, CUR))
                real, imag = product(T0, Y0 - b)
                real, imag = real + gf[b, 0], imag + gf[b, 1]
                if b < BLOCKS - 1:
                    split_store(CUR, real, imag)
                publish(second, b, real, imag)

        @pl.when(direction == 1)
        def _():
            for b in reversed(range(BLOCKS)):
                split_store(T0, *product(G0 - b, CUR))
                publish(second, b, *product(T0, G0 - b))
                if b > 0:
                    real, imag = product(CUR, X0 - b)
                    split_store(T1, real + af[b, 0], imag + af[b, 1])
                    split_store(CUR, *product(Y0 - b, T1))

    for i in range(2):
        for side in range(2):
            @pl.when(high == side)
            def _():
                chain((i + side) % 2, i == 0)

        if i == 0:
            pl.semaphore_wait(barrier, ne + neighbours)

        @pl.when(lax.rem(i + high, 2) == c)
        def _():
            swap_source.start()

        if i == 0:
            swap_p.start()
            swap_q.start()

        if i == 1:
            @pl.when(k == 1)
            def _():
                pass_on()

        @pl.when(lax.rem(i + high + c, 2) == 1)
        def _():
            join()

        if i == 0:
            compose()
            send_screened()

    @pl.loop(2, 4)
    def _(i):
        @pl.when(i == k)
        def _():
            pass_on()

        sweep(i - 2, lax.rem(i + high, 2))

    transform_screened()

    def own_self(b):
        return pltpu.make_async_copy(
            res.at[b, me], self_hbm.at[b, :, rows_of(me), :], out_sem.at[1, b]
        )

    @pl.loop(0, BLOCKS)
    def _(j):
        b = high * j + (1 - high) * (BLOCKS - 1 - j)
        batch(b, a_recv).wait()
        for r, v in tiles:
            at = (pl.ds(r, 8), pl.ds(v, 128))
            values = dft([(rows[(b, e, 0) + at], rows[(b, e, 1) + at]) for e in range(ne)])
            mixed = []
            for e in range(ne):
                vr, vi = values[e]
                wr, wi = srows[(e, b, 0) + at], srows[(e, b, 1) + at]
                mixed.append((vr * wi + vi * wr, vr * wr - vi * wi))
            values = dft(mixed)
            for e in range(ne):
                res[(b, e, 0) + at] = values[e][1]
                res[(b, e, 1) + at] = values[e][0]

        @pl.loop(0, ne - 1)
        def _(turn):
            to = peer(turn)
            pltpu.make_async_remote_copy(
                src_ref=res.at[b, to],
                dst_ref=self_hbm.at[b, :, rows_of(me), :],
                send_sem=r_send.at[b],
                recv_sem=r_recv.at[b],
                device_id=(seg, to),
                device_id_type=MESH,
            ).start()

        own_self(b).start()

    @pl.loop(0, BLOCKS)
    def _(b):
        for sem in (a_send, r_send, r_recv):
            batch(b, sem).wait()
        diag_out(b).wait()
        own_self(b).wait()

    spot = srows.at[pl.ds(0, ne - 1)]
    pltpu.make_async_copy(spot, spot, sc_sem.at[0]).wait()
    swap_source.wait_send()
    swap_p.wait_send()
    swap_q.wait_send()

    @pl.when(k < last)
    def _():
        for half in relay:
            half.wait_send()

    @pl.when(k > 0)
    def _():
        for half in forward:
            half.wait_send()


def hand_over(diag_in, self_in, diag_hbm, self_hbm, sem):
    copies = [
        pltpu.make_async_copy(src.at[b], dst.at[b], sem.at[j, b])
        for b in range(BLOCKS)
        for j, (src, dst) in enumerate(((diag_in, diag_hbm), (self_in, self_hbm)))
    ]
    for copy in copies:
        copy.start()
    for copy in copies:
        copy.wait()


def per_device(ny, nx, green, couple_left, couple_right, coupling, screened):
    shape = green.shape[1:]
    blocks, _, order, _ = shape
    ne = ny * nx
    depth = order // ne
    one = (2, order, order)
    anywhere = pl.BlockSpec(memory_space=pl.ANY)
    diagonal, self_energy = pl.pallas_call(
        functools.partial(kernel, ny, nx),
        out_shape=[jax.ShapeDtypeStruct(shape, F32)] * 2,
        in_specs=[anywhere] * 3 + [pl.BlockSpec(memory_space=pltpu.SMEM), anywhere],
        out_specs=[anywhere] * 2,
        scratch_shapes=[
            pltpu.VMEM(shape, F32),
            pltpu.VMEM(shape, F32),
            pltpu.VMEM(shape, F32),
            pltpu.VMEM((2,) + one, F32),
            pltpu.VMEM((2,) + one, F32),
            pltpu.VMEM((3,) + one, F32),
            pltpu.VMEM(one, F32),
            pltpu.VMEM(one, F32),
            pltpu.VMEM(one, F32),
            pltpu.VMEM(shape, F32),
            pltpu.VMEM((blocks, ne, 2, depth, order), F32),
            pltpu.VMEM((ne, blocks, 2, depth, order), F32),
            pltpu.VMEM((blocks, ne, 2, depth, order), F32),
            pltpu.VMEM((PLACES, 3, 2, order, order), BF16),
            pltpu.SemaphoreType.DMA((blocks, 3)),
            pltpu.SemaphoreType.DMA((3,)),
            pltpu.SemaphoreType.DMA((3,)),
            pltpu.SemaphoreType.DMA((3,)),
            pltpu.SemaphoreType.DMA((2, 2)),
            pltpu.SemaphoreType.DMA((2, 2)),
            pltpu.SemaphoreType.DMA((blocks,)),
            pltpu.SemaphoreType.DMA((blocks,)),
            pltpu.SemaphoreType.DMA((blocks,)),
            pltpu.SemaphoreType.DMA((blocks,)),
            pltpu.SemaphoreType.DMA((2, blocks)),
        ],
        compiler_params=pltpu.CompilerParams(
            collective_id=0, has_side_effects=True, vmem_limit_bytes=48 * 2**20
        ),
    )(green[0], couple_left[0], couple_right[0], coupling, screened[0])
    diagonal, self_energy = pl.pallas_call(
        hand_over,
        out_shape=[jax.ShapeDtypeStruct(shape, F32)] * 2,
        in_specs=[anywhere] * 2,
        out_specs=[anywhere] * 2,
        scratch_shapes=[pltpu.SemaphoreType.DMA((2, blocks))],
        compiler_params=pltpu.CompilerParams(vmem_limit_bytes=2**21),
    )(diagonal, self_energy)
    return diagonal[None], self_energy[None]


def solution(mesh):
    blocks = P("energy", "seg", None, None, None)
    energies = mesh.shape["energy"]
    nx = math.isqrt(energies)
    return jax.shard_map(
        functools.partial(per_device, energies // nx, nx),
        mesh=mesh,
        in_specs=(blocks, blocks, blocks, P("energy", "seg"), blocks),
        out_specs=(blocks, blocks),
        check_vma=False,
    )
```

```python
import functools
import math

import jax
import jax.numpy as jnp
from jax import lax
from jax.experimental import pallas as pl
from jax.experimental.pallas import tpu as pltpu
from jax.sharding import PartitionSpec as P

F32 = jnp.float32
BF16 = jnp.bfloat16
MESH = pl.DeviceIdType.MESH

G0, X0, Y0 = 3, 10, 17
T0, T1, A_IN, C_IN, RS, RP, RQ, U, W, M_IN, CUR = range(21, 32)
PLACES = 32
BLOCKS = 4


def dft(values):
    n = len(values)
    if n == 1:
        return values
    even, odd = dft(values[0::2]), dft(values[1::2])
    out = [None] * n
    half = n // 2
    for j in range(half):
        er, ei = even[j]
        orr, oi = odd[j]
        angle = -2.0 * math.pi * j / n
        cos, sin = math.cos(angle), math.sin(angle)
        if j == 0:
            tr, ti = orr, oi
        elif 4 * j == n:
            tr, ti = oi, -orr
        elif 8 * j == n:
            tr, ti = (orr + oi) * cos, (oi - orr) * cos
        elif 8 * j == 3 * n:
            tr, ti = (oi - orr) * -cos, (orr + oi) * cos
        else:
            tr, ti = orr * cos - oi * sin, orr * sin + oi * cos
        out[j] = (er + tr, ei + ti)
        out[j + half] = (er - tr, ei - ti)
    return out


def kernel(
    ny, nx,
    g_hbm, a_hbm, c_hbm, m_ref, w_hbm, diag_hbm, self_hbm,
    gf, af, cf, sf, pqf, rx, co, mi, oi, dg, rows, srows, res, ops,
    in_sem, sc_sem, x_send, x_recv, ch_sem, fw_sem, a_send, a_recv, r_send, r_recv, out_sem,
):
    ne = ny * nx
    depth = dg.shape[2] // ne
    width = dg.shape[3]
    seg = lax.axis_index("seg")
    me = lax.axis_index("energy")
    z, c = lax.div(seg, 2), lax.rem(seg, 2)
    nz = lax.axis_size("seg") // 2
    last = nz - 1
    my_y, my_x = lax.div(me, nx), lax.rem(me, nx)
    k = c * z + (1 - c) * (last - z)
    partner = seg + 1 - 2 * c
    onward = seg + 4 * c - 2
    high = lax.div(2 * z, nz)

    def stride(j, n):
        return lax.rem(2 - j + 3 * lax.div(j, 2) - 2 * lax.div(j, 3), 4) if n == 4 else n - 1 - j

    def peer(turn):
        dy, dx = stride(lax.div(turn, nx), ny), stride(lax.rem(turn, nx), nx)
        return lax.rem(my_y + dy, ny) * nx + lax.rem(my_x + dx, nx)

    def rows_of(energy):
        return pl.ds(pl.multiple_of(energy * depth, depth), depth)

    def load(b):
        return [
            pltpu.make_async_copy(src.at[b], dst.at[b], in_sem.at[b, j])
            for j, (src, dst) in enumerate(((g_hbm, gf), (a_hbm, af), (c_hbm, cf)))
        ]

    for b in range(BLOCKS):
        for copy in load(b):
            copy.start()

    barrier = pltpu.get_barrier_semaphore()

    pl.semaphore_signal(barrier, inc=1, device_id=(partner, me), device_id_type=MESH)

    @pl.when(z > 0)
    def _():
        pl.semaphore_signal(barrier, inc=1, device_id=(seg - 2, me), device_id_type=MESH)

    @pl.when(z < last)
    def _():
        pl.semaphore_signal(barrier, inc=1, device_id=(seg + 2, me), device_id_type=MESH)

    def split_store(place, real, imag, rows_in=slice(None)):
        for q, value in enumerate((real, imag, real + imag)):
            top = value.astype(BF16)
            ops[place, q, 0, rows_in] = top
            ops[place, q, 1, rows_in] = (value - top.astype(F32)).astype(BF16)

    def product(left, right, rows_in=slice(None), inner=slice(None)):
        parts = []
        for q in range(3):
            lhs = [ops[left, q, part, rows_in, inner] for part in (0, 0, 1)]
            rhs = [ops[right, q, part, inner] for part in (0, 1, 0)]
            parts.append(
                jnp.dot(
                    jnp.concatenate(lhs, axis=1),
                    jnp.concatenate(rhs, axis=0),
                    preferred_element_type=F32,
                )
            )
        return parts[0] - parts[1], parts[2] - parts[0] - parts[1]

    dg[...] = jnp.zeros(dg.shape, F32)
    for b in range(BLOCKS):
        for copy in load(b):
            copy.wait()
        weight = m_ref[0, b].astype(F32)
        af[b] = af[b] * weight
        split_store(G0 - b, gf[b, 0], gf[b, 1])
        split_store(A_IN, af[b, 0], af[b, 1])
        split_store(C_IN, cf[b, 0], cf[b, 1])
        for energy in range(b * (ne - 1) // BLOCKS, (b + 1) * (ne - 1) // BLOCKS):
            other = lax.rem(me + 1 + energy, ne)
            pl.semaphore_signal(barrier, inc=1, device_id=(seg, other), device_id_type=MESH)
        split_store(X0 - b, *product(G0 - b, A_IN))
        split_store(Y0 - b, *product(C_IN, G0 - b))

    neighbours = lax.div(z + last, nz) + lax.div(last - z + last, nz)
    own_screen = pltpu.make_async_copy(w_hbm.at[:, :, rows_of(me), :], srows.at[me], sc_sem.at[2])
    own_screen.start()

    def send_screened():
        @pl.loop(0, ne - 1)
        def _(turn):
            to = peer(turn)
            pltpu.make_async_remote_copy(
                src_ref=w_hbm.at[:, :, rows_of(to), :],
                dst_ref=srows.at[me],
                send_sem=sc_sem.at[0],
                recv_sem=sc_sem.at[1],
                device_id=(seg, to),
                device_id_type=MESH,
            ).start()

    def exchange(j, src):
        return pltpu.make_async_remote_copy(
            src_ref=src,
            dst_ref=rx.at[j],
            send_sem=x_send.at[j],
            recv_sem=x_recv.at[j],
            device_id=(partner, me),
            device_id_type=MESH,
        )

    swap_source = exchange(0, sf.at[c])
    swap_p, swap_q = exchange(1, pqf.at[0]), exchange(2, pqf.at[1])

    own_p, own_q = X0 + BLOCKS - 1, Y0 + BLOCKS - 1
    own_left = c * own_p + (1 - c) * own_q
    own_right = c * own_q + (1 - c) * own_p
    his_left = RP + 1 - c
    his_right = RP + c
    order = dg.shape[2]
    halves = [slice(h * order // 2, (h + 1) * order // 2) for h in range(2)]
    relay = [
        pltpu.make_async_remote_copy(
            src_ref=co.at[:, half], dst_ref=mi.at[:, half],
            send_sem=ch_sem.at[0, h], recv_sem=ch_sem.at[1, h],
            device_id=(onward, me), device_id_type=MESH,
        )
        for h, half in enumerate(halves)
    ]
    forward = [
        pltpu.make_async_remote_copy(
            src_ref=mi.at[:, half], dst_ref=oi.at[:, half],
            send_sem=fw_sem.at[0, h], recv_sem=fw_sem.at[1, h],
            device_id=(partner, me), device_id_type=MESH,
        )
        for h, half in enumerate(halves)
    ]

    def chain(direction, outer):
        for b in range(BLOCKS):
            j = BLOCKS - 1 - b
            if direction == 0 and b > 0:
                split_store(T0, *product(X0 - b, G0 + b - 1))
            if direction == 1 and b == 0:
                split_store(T1, af[j, 0], af[j, 1])
            if direction == 1 and b > 0:
                real, imag = product(CUR, X0 - j)
                split_store(T1, real + af[j, 0], imag + af[j, 1])
            if outer and 0 < b < BLOCKS - 1:
                split_store(X0 + b, *product(X0 - b, X0 + b - 1))
            if direction == 0 and b > 0:
                real, imag = product(T0, Y0 - b)
                real, imag = real + gf[b, 0], imag + gf[b, 1]
                if b < BLOCKS - 1:
                    split_store(G0 + b, real, imag)
            if direction == 1:
                real, imag = product(Y0 - j, T1)
                if b < BLOCKS - 1:
                    split_store(CUR, real, imag)
            if b == BLOCKS - 1:
                sf[direction, 0] = real
                sf[direction, 1] = imag
                if outer:
                    pl.semaphore_wait(barrier, ne + neighbours)

                @pl.when(c == direction)
                def _():
                    swap_source.start()

            if outer and b == BLOCKS - 1:
                real, imag = product(X0 - b, X0 + b - 1)
                pqf[0, 0] = real
                pqf[0, 1] = imag
                split_store(X0 + b, real, imag)
            if outer and b > 0:
                real, imag = product(Y0 + b - 1, Y0 - b)
                if b == BLOCKS - 1:
                    pqf[1, 0] = real
                    pqf[1, 1] = imag
                split_store(Y0 + b, real, imag)

    def join():
        swap_source.wait_recv()
        split_store(RS, rx[0, 0], rx[0, 1])
        split_store(T0, *product(own_left, RS))
        for h, half in enumerate(halves):
            real, imag = product(T0, own_right, half)
            co[0, half] = real + sf[1 - c, 0, half]
            co[1, half] = imag + sf[1 - c, 1, half]

            @pl.when(k == 0)
            def _():
                relay[h].start()

    def compose():
        swap_p.wait_recv()
        swap_q.wait_recv()
        split_store(RP, rx[1, 0], rx[1, 1])
        split_store(RQ, rx[2, 0], rx[2, 1])

        @pl.when(k < last)
        def _():
            split_store(U, *product(own_left, his_left))
            split_store(W, *product(his_right, own_right))

        @pl.when(k == last)
        def _():
            ops[U] = ops[his_left]
            ops[W] = ops[his_right]

    def batch(b, sem):
        spot = rows.at[b, pl.ds(0, ne - 1)]
        return pltpu.make_async_copy(spot, spot, sem.at[b])

    def diag_out(b):
        return pltpu.make_async_copy(dg.at[b], diag_hbm.at[b], out_sem.at[0, b])

    def publish(second, b, real, imag):
        dg[b, 0] = dg[b, 0] + real
        dg[b, 1] = dg[b, 1] + imag

        @pl.when(second == 1)
        def _():
            @pl.loop(0, ne - 1)
            def _(turn):
                to = peer(turn)
                pltpu.make_async_remote_copy(
                    src_ref=dg.at[b, :, rows_of(to), :],
                    dst_ref=rows.at[b, me],
                    send_sem=a_send.at[b],
                    recv_sem=a_recv.at[b],
                    device_id=(seg, to),
                    device_id_type=MESH,
                ).start()

            diag_out(b).start()
            rows[b, me] = dg[b, :, rows_of(me), :]

    tiles = [(r, v) for r in range(0, depth, 8) for v in range(0, width, 128)]

    def transform_screened():
        spot = srows.at[pl.ds(0, ne - 1)]
        pltpu.make_async_copy(spot, spot, sc_sem.at[1]).wait()
        own_screen.wait()

        @pl.loop(0, BLOCKS)
        def _(b):
            for r, v in tiles:
                at = (pl.ds(r, 8), pl.ds(v, 128))
                values = dft([(srows[(e, b, 0) + at], srows[(e, b, 1) + at]) for e in range(ne)])
                for e in range(ne):
                    srows[(e, b, 0) + at] = values[e][0] * (1.0 / ne)
                    srows[(e, b, 1) + at] = values[e][1] * (1.0 / ne)

    def pass_on():
        @pl.when(k == last)
        def _():
            co[...] = rx[0]

        for h, half in enumerate(halves):
            relay[h].wait_recv()
            forward[h].start()
            split_store(M_IN, mi[0, half], mi[1, half], half)
            split_store(T0, *product(M_IN, W, half), half)
            for g, other in enumerate(halves):
                real, imag = product(U, T0, other, half)
                co[0, other] = co[0, other] + real
                co[1, other] = co[1, other] + imag
                if h == 1:
                    @pl.when(k < last)
                    def _():
                        relay[g].start()

    def sweep(second, direction):
        own = lax.rem(direction + c, 2) == 1

        @pl.when(own & (k == last))
        def _():
            split_store(CUR, co[0], co[1])

        @pl.when(own & (k > 0) & (k < last))
        def _():
            split_store(T0, *product(his_left, M_IN))
            real, imag = product(T0, his_right)
            split_store(CUR, real + rx[0, 0], imag + rx[0, 1])

        @pl.when(own & (k == 0))
        def _():
            split_store(CUR, rx[0, 0], rx[0, 1])

        @pl.when(jnp.logical_not(own) & (k < last))
        def _():
            for copy, half in zip(forward, halves):
                copy.wait_recv()
                split_store(CUR, oi[0, half], oi[1, half], half)

        @pl.when(jnp.logical_not(own) & (k == last))
        def _():
            ops[CUR] = jnp.zeros(ops.shape[1:], BF16)

        @pl.when(direction == 0)
        def _():
            for b in range(BLOCKS):
                split_store(T0, *product(X0 - b, CUR))
                real, imag = product(T0, Y0 - b)
                real, imag = real + gf[b, 0], imag + gf[b, 1]
                if b < BLOCKS - 1:
                    split_store(CUR, real, imag)
                publish(second, b, real, imag)

        @pl.when(direction == 1)
        def _():
            for b in reversed(range(BLOCKS)):
                split_store(T0, *product(G0 - b, CUR))
                publish(second, b, *product(T0, G0 - b))
                if b > 0:
                    real, imag = product(CUR, X0 - b)
                    split_store(T1, real + af[b, 0], imag + af[b, 1])
                    split_store(CUR, *product(Y0 - b, T1))

    for i in range(2):
        for side in range(2):
            @pl.when(high == side)
            def _():
                chain((i + side) % 2, i == 0)

        if i == 0:
            swap_p.start()
            swap_q.start()

        if i == 1:
            @pl.when(k == 1)
            def _():
                pass_on()

        @pl.when(lax.rem(i + high + c, 2) == 1)
        def _():
            join()

        if i == 0:
            compose()
            send_screened()

    @pl.loop(2, 4)
    def _(i):
        @pl.when(i == k)
        def _():
            pass_on()

        sweep(i - 2, lax.rem(i + high, 2))

    transform_screened()

    def own_self(b):
        return pltpu.make_async_copy(
            res.at[b, me], self_hbm.at[b, :, rows_of(me), :], out_sem.at[1, b]
        )

    @pl.loop(0, BLOCKS)
    def _(j):
        b = high * j + (1 - high) * (BLOCKS - 1 - j)
        batch(b, a_recv).wait()
        for r, v in tiles:
            at = (pl.ds(r, 8), pl.ds(v, 128))
            values = dft([(rows[(b, e, 0) + at], rows[(b, e, 1) + at]) for e in range(ne)])
            mixed = []
            for e in range(ne):
                vr, vi = values[e]
                wr, wi = srows[(e, b, 0) + at], srows[(e, b, 1) + at]
                mixed.append((vr * wi + vi * wr, vr * wr - vi * wi))
            values = dft(mixed)
            for e in range(ne):
                res[(b, e, 0) + at] = values[e][1]
                res[(b, e, 1) + at] = values[e][0]

        @pl.loop(0, ne - 1)
        def _(turn):
            to = peer(turn)
            pltpu.make_async_remote_copy(
                src_ref=res.at[b, to],
                dst_ref=self_hbm.at[b, :, rows_of(me), :],
                send_sem=r_send.at[b],
                recv_sem=r_recv.at[b],
                device_id=(seg, to),
                device_id_type=MESH,
            ).start()

        own_self(b).start()

    @pl.loop(0, BLOCKS)
    def _(b):
        for sem in (a_send, r_send, r_recv):
            batch(b, sem).wait()
        diag_out(b).wait()
        own_self(b).wait()

    spot = srows.at[pl.ds(0, ne - 1)]
    pltpu.make_async_copy(spot, spot, sc_sem.at[0]).wait()
    swap_source.wait_send()
    swap_p.wait_send()
    swap_q.wait_send()

    @pl.when(k < last)
    def _():
        for half in relay:
            half.wait_send()

    @pl.when(k > 0)
    def _():
        for half in forward:
            half.wait_send()


def hand_over(diag_in, self_in, diag_hbm, self_hbm, sem):
    copies = [
        pltpu.make_async_copy(src.at[b], dst.at[b], sem.at[j, b])
        for b in range(BLOCKS)
        for j, (src, dst) in enumerate(((diag_in, diag_hbm), (self_in, self_hbm)))
    ]
    for copy in copies:
        copy.start()
    for copy in copies:
        copy.wait()


def per_device(ny, nx, green, couple_left, couple_right, coupling, screened):
    shape = green.shape[1:]
    blocks, _, order, _ = shape
    ne = ny * nx
    depth = order // ne
    one = (2, order, order)
    anywhere = pl.BlockSpec(memory_space=pl.ANY)
    diagonal, self_energy = pl.pallas_call(
        functools.partial(kernel, ny, nx),
        out_shape=[jax.ShapeDtypeStruct(shape, F32)] * 2,
        in_specs=[anywhere] * 3 + [pl.BlockSpec(memory_space=pltpu.SMEM), anywhere],
        out_specs=[anywhere] * 2,
        scratch_shapes=[
            pltpu.VMEM(shape, F32),
            pltpu.VMEM(shape, F32),
            pltpu.VMEM(shape, F32),
            pltpu.VMEM((2,) + one, F32),
            pltpu.VMEM((2,) + one, F32),
            pltpu.VMEM((3,) + one, F32),
            pltpu.VMEM(one, F32),
            pltpu.VMEM(one, F32),
            pltpu.VMEM(one, F32),
            pltpu.VMEM(shape, F32),
            pltpu.VMEM((blocks, ne, 2, depth, order), F32),
            pltpu.VMEM((ne, blocks, 2, depth, order), F32),
            pltpu.VMEM((blocks, ne, 2, depth, order), F32),
            pltpu.VMEM((PLACES, 3, 2, order, order), BF16),
            pltpu.SemaphoreType.DMA((blocks, 3)),
            pltpu.SemaphoreType.DMA((3,)),
            pltpu.SemaphoreType.DMA((3,)),
            pltpu.SemaphoreType.DMA((3,)),
            pltpu.SemaphoreType.DMA((2, 2)),
            pltpu.SemaphoreType.DMA((2, 2)),
            pltpu.SemaphoreType.DMA((blocks,)),
            pltpu.SemaphoreType.DMA((blocks,)),
            pltpu.SemaphoreType.DMA((blocks,)),
            pltpu.SemaphoreType.DMA((blocks,)),
            pltpu.SemaphoreType.DMA((2, blocks)),
        ],
        compiler_params=pltpu.CompilerParams(
            collective_id=0, has_side_effects=True, vmem_limit_bytes=48 * 2**20
        ),
    )(green[0], couple_left[0], couple_right[0], coupling, screened[0])
    diagonal, self_energy = pl.pallas_call(
        hand_over,
        out_shape=[jax.ShapeDtypeStruct(shape, F32)] * 2,
        in_specs=[anywhere] * 2,
        out_specs=[anywhere] * 2,
        scratch_shapes=[pltpu.SemaphoreType.DMA((2, blocks))],
        compiler_params=pltpu.CompilerParams(vmem_limit_bytes=2**21),
    )(diagonal, self_energy)
    return diagonal[None], self_energy[None]


def solution(mesh):
    blocks = P("energy", "seg", None, None, None)
    energies = mesh.shape["energy"]
    nx = math.isqrt(energies)
    return jax.shard_map(
        functools.partial(per_device, energies // nx, nx),
        mesh=mesh,
        in_specs=(blocks, blocks, blocks, P("energy", "seg"), blocks),
        out_specs=(blocks, blocks),
        check_vma=False,
    )
```
